128 devices in a mesh: ctx: 32 (over x, y, z_hi), wsh: 4 (over z_lo, core).
Axes of the slice: x: 4, y: 4, z: 4 (z_hi: 2, z_lo: 2; z = z_hi * 2 + z_lo), core: 2. Of those that a mesh axis runs over, the one named last changes fastest.
Arguments:
- tokens: bfloat16 [4, 4096, 1024], P('wsh', 'ctx'), may hold values from -6 to 6
- places: int32 [4, 4096], P('wsh', 'ctx'), may hold values from 0 to 4095, as said below
- w_qkv: bfloat16 [1024, 3072], P('wsh'), may hold values from -0.1875 to 0.1875
- b_qv: bfloat16 [2048], P('wsh'), may hold values from -3 to 3
- w_out: bfloat16 [1024, 1024], P('wsh'), may hold values from -0.5 to 0.5
- b_out: bfloat16 [1024], P('wsh'), may hold values from -3 to 3
- norm1_gain: bfloat16 [1024], P('wsh'), may hold values from 0.5 to 1.5
- norm1_shift: bfloat16 [1024], P('wsh'), may hold values from -3 to 3
- norm2_gain: bfloat16 [1024], P('wsh'), may hold values from 0.5 to 1.5
- norm2_shift: bfloat16 [1024], P('wsh'), may hold values from -3 to 3
- w_up: bfloat16 [1024, 4096], P('wsh'), may hold values from -0.1875 to 0.1875
- b_up: bfloat16 [4096], P('wsh'), may hold values from -3 to 3
- w_down: bfloat16 [4096, 1024], P('wsh'), may hold values from -0.09375 to 0.09375
- b_down: bfloat16 [1024], P('wsh'), may hold values from -3 to 3
- cotangent: bfloat16 [4, 4096, 1024], P('wsh', 'ctx'), may hold values from -6 to 6
Outputs:
- output: bfloat16 [4, 4096, 1024], P('wsh', 'ctx')
- grad_tokens: bfloat16 [4, 4096, 1024], P('wsh', 'ctx')
- grad_w_qkv: float32 [1024, 3072], P('wsh')
- grad_b_qv: float32 [2048], P('wsh')
- grad_w_out: float32 [1024, 1024], P('wsh')
- grad_b_out: float32 [1024], P('wsh')
- grad_norm1_gain: float32 [1024], P('wsh')
- grad_norm1_shift: float32 [1024], P('wsh')
- grad_norm2_gain: float32 [1024], P('wsh')
- grad_norm2_shift: float32 [1024], P('wsh')
- grad_w_up: float32 [1024, 4096], P('wsh')
- grad_b_up: float32 [4096], P('wsh')
- grad_w_down: float32 [4096, 1024], P('wsh')
- grad_b_down: float32 [1024], P('wsh')
The draws below stay inside these ranges and needn't reach their ends.
Inputs may be any that keep to these rules, and one draw needn't show every extreme that they name: `places`: within each sequence every position appears once; each device's 128 stored tokens along ctx are two runs of 64 consecutive positions, the run starting at b * 64 followed by the run starting at 4096 - (b + 1) * 64, with b different on every device of the sequence.
All inputs are finite; a program needn't handle non-finite values.
Results may differ from the reference program's by a relative error of at most 0.04.
Values may be sent and summed in bfloat16 or wider, within the bound.
No kernel may reach another device: no remote copies, remote signals or barrier semaphores. Data moves between devices by JAX's collectives and lax.ppermute only.
A program may use at most 192 MiB of HBM per device.

```python
import jax
import jax.numpy as jnp
from jax import lax

HEADS = 16
HEAD_DIM = 64
FF = 4096
D = 1024
HALF = 64
SEQ_LEN = 4096
SEQS = 4


def draw_places(key, part):
    key = jax.random.fold_in(key, 7)
    blocks = SEQ_LEN // HALF
    devices = blocks // 2

    def one_sequence(index):
        order = jax.random.permutation(jax.random.fold_in(key, index), devices).astype(jnp.int32)
        offsets = jnp.arange(HALF, dtype=jnp.int32)
        early = order[:, None] * HALF + offsets[None, :]
        late = (blocks - 1 - order)[:, None] * HALF + offsets[None, :]
        return jnp.concatenate([early, late], axis=1).reshape(SEQ_LEN).astype(jnp.int32)
    return jax.vmap(one_sequence)(jnp.arange(SEQS, dtype=jnp.int32))


def level_of(own_key, shape, cuts, least, top_value):
    level, own = 1.0, jax.random.fold_in(own_key, 6)
    for axis_at, shards_of in cuts:
        draws = jnp.exp(jax.random.uniform(jax.random.fold_in(own, axis_at), (shards_of,), jnp.float32, least / len(cuts), top_value / len(cuts)))
        level = level * jnp.repeat(draws, shape[axis_at] // shards_of).reshape([-1 if axis == axis_at else 1 for axis in range(len(shape))])
    return level


def noise(own_key, shape, deviation, reach, shards=(), kind=jnp.bfloat16):
    drawn = deviation * jax.random.normal(own_key, shape, jnp.float32)
    if shards:
        drawn = drawn * level_of(own_key, shape, shards, -0.22, 0.18)
    return jnp.clip(drawn, -reach, reach).astype(kind)


def setup_inputs(seed: int = 0) -> dict:
    splits = jax.random.split(jax.random.key(seed), 16)
    return {
        "tokens": noise(splits[0], (SEQS, SEQ_LEN, D), 1.0, 6.0, ((0, 4), (1, 32))),
        "places": draw_places(jax.random.fold_in(splits[15], 71), 0),
        "w_qkv": noise(splits[2], (D, 3 * D), D ** -0.5, 0.1875, ((0, 4),)),
        "b_qv": noise(splits[3], (2 * D,), 0.5, 3.0, ((0, 4),)),
        "w_out": noise(splits[4], (D, D), (2 * HEAD_DIM) ** -0.5, 0.5, ((0, 4),)),
        "b_out": noise(splits[5], (D,), 0.5, 3.0, ((0, 4),)),
        "norm1_gain": jnp.clip(1.0 + 0.1 * jax.random.normal(splits[6], (D,), jnp.float32), 0.5, 1.5).astype(jnp.bfloat16),
        "norm1_shift": noise(splits[7], (D,), 0.5, 3.0, ((0, 4),)),
        "norm2_gain": jnp.clip(1.0 + 0.1 * jax.random.normal(splits[8], (D,), jnp.float32), 0.5, 1.5).astype(jnp.bfloat16),
        "norm2_shift": noise(splits[9], (D,), 0.5, 3.0, ((0, 4),)),
        "w_up": noise(splits[10], (D, FF), D ** -0.5, 0.1875, ((0, 4),)),
        "b_up": noise(splits[11], (FF,), 0.5, 3.0, ((0, 4),)),
        "w_down": noise(splits[12], (FF, D), FF ** -0.5, 0.09375, ((0, 4),)),
        "b_down": noise(splits[13], (D,), 0.5, 3.0, ((0, 4),)),
        "cotangent": noise(splits[14], (SEQS, SEQ_LEN, D), 1.0, 6.0, ((0, 4), (1, 32))),
    }


EPS = 1e-05
HIGHEST = lax.Precision.HIGHEST

@jax.custom_vjp
def low(v):
    return lax.optimization_barrier(v.astype(jnp.bfloat16)).astype(jnp.float32)

@jax.custom_vjp
def low_back(v):
    return v

def low_keep(v):
    return (low(v), None)

def low_pass(kept, grad):
    return (grad,)

def back_keep(v):
    return (v, None)

def back_low(kept, grad):
    return (low(grad),)
low.defvjp(low_keep, low_pass)
low_back.defvjp(back_keep, back_low)

def layer_norm(values, gain_vec, shift_vec):
    average = lax.optimization_barrier(jnp.mean(values, axis=-1, keepdims=True))
    centred = values - average
    variance = lax.optimization_barrier(jnp.mean(centred * centred, axis=-1, keepdims=True))
    return centred * lax.rsqrt(variance + EPS) * gain_vec + shift_vec

def gelu_tanh(values):
    return 0.5 * values * (1.0 + jnp.tanh(0.7978845608028654 * (values + 0.044715 * values * values * values)))

def product(left, right):
    return jnp.dot(left, right, precision=HIGHEST, preferred_element_type=jnp.float32)

def attend_block(query, keys, values, query_places, key_places, slopes):
    rows = query.shape[0]
    key_rows = keys.shape[0]
    q_heads = query.reshape(rows, HEADS, HEAD_DIM)
    k_heads = keys.reshape(key_rows, HEADS, HEAD_DIM)
    v_heads = values.reshape(key_rows, HEADS, HEAD_DIM)
    scores = jnp.einsum('qhd,khd->hqk', q_heads, k_heads, precision=HIGHEST) * HEAD_DIM ** (-0.5)
    distance = (query_places[:, None] - key_places[None, :]).astype(jnp.float32)
    scores = low_back(scores - slopes[:, None, None] * distance[None, :, :])
    allowed = (key_places[None, :] <= query_places[:, None])[None, :, :]
    masked = jnp.where(allowed, scores, -1e+30)
    highest = lax.optimization_barrier(jnp.max(masked, axis=-1, keepdims=True))
    weights = jnp.where(allowed, jnp.exp(masked - highest), 0.0)
    weights = low(weights / lax.optimization_barrier(jnp.sum(weights, axis=-1, keepdims=True)))
    mixed = jnp.einsum('hqk,khd->qhd', weights, v_heads, precision=HIGHEST)
    return mixed.reshape(rows, HEADS * HEAD_DIM)

def sequence_forward(tokens, places, params):
    w_qkv, b_qv, w_out, b_out, gain_one, shift_one, gain_two, shift_two, w_up, b_up, w_down, b_down = params
    width = HEADS * HEAD_DIM
    length = tokens.shape[0]
    slopes = 8.0 * jnp.exp2(-4.0 * (jnp.arange(HEADS, dtype=jnp.float32) + 1.0) / HEADS) / length
    normed = low(layer_norm(tokens, gain_one, shift_one))
    mixed = product(normed, w_qkv)
    query = low(low_back(mixed[:, :width] + b_qv[:width]))
    keys = low(low_back(mixed[:, width:2 * width]))
    values = low(low_back(mixed[:, 2 * width:] + b_qv[width:]))
    block = min(512, length)
    count_blocks = length // block

    def one_block(inputs):
        return attend_block(inputs[0], keys, values, inputs[1], places, slopes)
    attended = lax.map(jax.checkpoint(one_block), (query.reshape(count_blocks, block, width), places.reshape(count_blocks, block)))
    attended = low(low_back(attended.reshape(length, width)))
    middle = tokens + low_back(product(attended, w_out) + b_out)
    normed_two = low(layer_norm(middle, gain_two, shift_two))
    pre_act = low_back(product(normed_two, w_up) + b_up)
    hidden = low(gelu_tanh(pre_act))
    return middle + low_back(product(hidden, w_down) + b_down)

def reference(tokens, places, w_qkv, b_qv, w_out, b_out, norm1_gain, norm1_shift, norm2_gain, norm2_shift, w_up, b_up, w_down, b_down, cotangent):
    params = tuple((item.astype(jnp.float32) for item in (w_qkv, b_qv, w_out, b_out, norm1_gain, norm1_shift, norm2_gain, norm2_shift, w_up, b_up, w_down, b_down)))

    def whole(inputs, weights):

        def one_sequence(pair):
            return sequence_forward(pair[0], pair[1], weights)
        return lax.map(one_sequence, (inputs, places))
    output, pullback = jax.vjp(whole, tokens.astype(jnp.float32), params)
    grad_tokens, grads = pullback(cotangent.astype(jnp.float32))
    return (output.astype(jnp.bfloat16), grad_tokens.astype(jnp.bfloat16), grads[0], grads[1], grads[2], grads[3], grads[4], grads[5], grads[6], grads[7], grads[8], grads[9], grads[10], grads[11])
```

```python
import functools

import jax
import jax.numpy as jnp
from jax import lax
from jax.experimental import pallas as pl
from jax.experimental.pallas import tpu as pltpu
from jax.sharding import PartitionSpec as P

HEADS = 16
HEAD_DIM = 64
EPS = 1e-05
NEGATIVE = -1e30
RUN = 64
Q_TILE = 256
K_TILE = 512
F32 = jnp.float32
BF16 = jnp.bfloat16
VMEM = pl.BlockSpec(memory_space=pltpu.VMEM)
SMEM = pl.BlockSpec(memory_space=pltpu.SMEM)
PARAMS = pltpu.CompilerParams(vmem_limit_bytes=48 * 1024 * 1024)


def layer_norm(values, gain_vec, shift_vec):
    average = jnp.mean(values, axis=-1, keepdims=True)
    centred = values - average
    variance = jnp.mean(centred * centred, axis=-1, keepdims=True)
    return centred * lax.rsqrt(variance + EPS) * gain_vec + shift_vec


def gelu_tanh(values):
    return (
        0.5
        * values
        * (1.0 + jnp.tanh(0.7978845608028654 * (values + 0.044715 * values * values * values)))
    )


def dot(left, right, left_dim, right_dim):
    return lax.dot_general(
        left, right, (((left_dim,), (right_dim,)), ((), ())), preferred_element_type=F32
    )


def pack_qkv_kernel(mixed_ref, bias_ref, out_ref):
    for slot in range(4):
        for head in range(4):
            parts = [[], []]
            for half in range(2):
                rows = pl.ds(slot * 128 + half * RUN, RUN)
                for part in range(3):
                    cols = pl.ds(part * 256 + head * HEAD_DIM, HEAD_DIM)
                    parts[half].append(mixed_ref[rows, cols] + bias_ref[:, cols])
            (qe, ke, ve), (ql, kl, vl) = parts
            out_ref[slot * 4 + head] = jnp.concatenate([qe, ql, ke, ve, kl, vl], axis=1).astype(
                BF16
            )


def pack_qkv(mixed, bias):
    return pl.pallas_call(
        pack_qkv_kernel,
        out_shape=jax.ShapeDtypeStruct((16, RUN, 384), BF16),
        in_specs=[VMEM, VMEM],
        out_specs=VMEM,
        compiler_params=PARAMS,
    )(mixed, bias)


def pack_heads_kernel(flat_ref, out_ref):
    for slot in range(4):
        for head in range(4):
            cols = pl.ds(head * HEAD_DIM, HEAD_DIM)
            out_ref[slot * 4 + head] = jnp.concatenate(
                [
                    flat_ref[pl.ds(slot * 128, RUN), cols],
                    flat_ref[pl.ds(slot * 128 + RUN, RUN), cols],
                ],
                axis=1,
            ).astype(BF16)


def pack_heads(flat):
    return pl.pallas_call(
        pack_heads_kernel,
        out_shape=jax.ShapeDtypeStruct((16, RUN, 128), BF16),
        in_specs=[VMEM],
        out_specs=VMEM,
        compiler_params=PARAMS,
    )(flat)


def unpack_heads_kernel(packed_ref, out_ref):
    for slot in range(4):
        for half in range(2):
            rows = pl.ds(slot * 128 + half * RUN, RUN)
            out_ref[rows, :] = jnp.concatenate(
                [
                    packed_ref[slot * 4 + head, :, pl.ds(half * HEAD_DIM, HEAD_DIM)]
                    for head in range(4)
                ],
                axis=1,
            )


def unpack_heads(packed):
    return pl.pallas_call(
        unpack_heads_kernel,
        out_shape=jax.ShapeDtypeStruct((512, 256), BF16),
        in_specs=[VMEM],
        out_specs=VMEM,
        compiler_params=PARAMS,
    )(packed)


def unpack_qkv_kernel(packed_ref, out_ref):
    starts = ((0, 128, 192), (64, 256, 320))
    for slot in range(4):
        for half in range(2):
            rows = pl.ds(slot * 128 + half * RUN, RUN)
            out_ref[rows, :] = jnp.concatenate(
                [
                    packed_ref[slot * 4 + head, :, pl.ds(starts[half][part], HEAD_DIM)]
                    for part in range(3)
                    for head in range(4)
                ],
                axis=1,
            )


def unpack_qkv(packed):
    return pl.pallas_call(
        unpack_qkv_kernel,
        out_shape=jax.ShapeDtypeStruct((512, 768), BF16),
        in_specs=[VMEM],
        out_specs=VMEM,
        compiler_params=PARAMS,
    )(packed)


def run_rows(index):
    return pl.ds(pl.multiple_of(index * RUN, RUN), RUN)


def query_places(sorted_ref, tile):
    lane = lax.broadcasted_iota(jnp.int32, (1, Q_TILE), 1)
    base = jnp.zeros((1, Q_TILE), jnp.int32)
    for block in range(Q_TILE // RUN):
        start = sorted_ref[tile * (Q_TILE // RUN) + block] * RUN - block * RUN
        base = jnp.where(lane // RUN == block, start, base)
    return base + lane


def chunk_bounds(sorted_ref, tile):
    per = Q_TILE // RUN
    lowest = sorted_ref[tile * per] * RUN
    highest = sorted_ref[tile * per + per - 1] * RUN + RUN
    return lowest // K_TILE, (highest + K_TILE - 1) // K_TILE


def sort_queries(scalar_ref, sorted_ref):
    for index in range(32):
        sorted_ref[scalar_ref[index]] = scalar_ref[32 + index]


def attend_kernel(
    scalar_ref, slope_ref, own_ref, other_ref,
    out_ref, q_ref, k_ref, v_ref, exact_ref, log_ref,
    sorted_ref, vt_ref, rows_ref,
):
    sort_queries(scalar_ref, sorted_ref)
    for source in range(16):
        for half in range(2):
            index = source * 2 + half
            cols = half * HEAD_DIM
            q_ref[run_rows(scalar_ref[index]), :] = (
                own_ref[source, :, pl.ds(cols, HEAD_DIM)].astype(F32) * HEAD_DIM ** (-0.5)
            ).astype(BF16)
            place = run_rows(scalar_ref[32 + index])
            k_ref[place, :] = own_ref[source, :, pl.ds(128 + half * 128, HEAD_DIM)]
            v_ref[place, :] = own_ref[source, :, pl.ds(192 + half * 128, HEAD_DIM)]
            place = run_rows(scalar_ref[64 + index])
            k_ref[place, :] = other_ref[source, :, pl.ds(half * 128, HEAD_DIM)]
            v_ref[place, :] = other_ref[source, :, pl.ds(64 + half * 128, HEAD_DIM)]
    for chunk in range(4096 // K_TILE):
        rows = pl.ds(chunk * K_TILE, K_TILE)
        vt_ref[:, rows] = v_ref[rows, :].T
    slope = slope_ref[0]
    ramp = lax.broadcasted_iota(jnp.int32, (K_TILE, Q_TILE), 0)
    bias = ramp.astype(F32) * slope

    def tile_step(tile, unused):
        q_rows = pl.ds(pl.multiple_of(tile * Q_TILE, Q_TILE), Q_TILE)
        query = q_ref[q_rows, :]
        places = query_places(sorted_ref, tile)
        full, every = chunk_bounds(sorted_ref, tile)

        def chunk_step(masked, chunk, carry):
            highest, total, accum = carry
            k_rows = pl.ds(pl.multiple_of(chunk * K_TILE, K_TILE), K_TILE)
            scores = dot(k_ref[k_rows, :], query, 1, 1) + bias
            if masked:
                scores = jnp.where(ramp <= places - chunk * K_TILE, scores, NEGATIVE)
            offset = slope * (chunk * K_TILE).astype(F32)
            new_high = jnp.maximum(highest, jnp.max(scores, axis=0, keepdims=True) + offset)
            weights = jnp.exp(scores - (new_high - offset))
            factor = jnp.exp(highest - new_high)
            total = total * factor + jnp.sum(weights, axis=0, keepdims=True)
            accum = accum * factor + dot(vt_ref[:, k_rows], weights.astype(BF16), 1, 0)
            return new_high, total, accum

        carry = (
            jnp.full((1, Q_TILE), NEGATIVE, F32),
            jnp.zeros((1, Q_TILE), F32),
            jnp.zeros((HEAD_DIM, Q_TILE), F32),
        )
        carry = lax.fori_loop(0, full, functools.partial(chunk_step, False), carry)
        highest, total, accum = lax.fori_loop(
            full, every, functools.partial(chunk_step, True), carry
        )
        exact = accum / total
        exact_ref[:, q_rows] = exact
        log_ref[:, q_rows] = highest + jnp.log(total)
        rows_ref[q_rows, :] = exact.T
        return unused

    lax.fori_loop(0, 2048 // Q_TILE, tile_step, 0)
    for source in range(16):
        out_ref[source] = jnp.concatenate(
            [rows_ref[run_rows(scalar_ref[source * 2 + half]), :] for half in range(2)], axis=1
        ).astype(BF16)


def attend(scalars, slope, own, other):
    return pl.pallas_call(
        attend_kernel,
        out_shape=(
            jax.ShapeDtypeStruct((16, RUN, 128), BF16),
            jax.ShapeDtypeStruct((2048, HEAD_DIM), BF16),
            jax.ShapeDtypeStruct((4096, HEAD_DIM), BF16),
            jax.ShapeDtypeStruct((4096, HEAD_DIM), BF16),
            jax.ShapeDtypeStruct((HEAD_DIM, 2048), F32),
            jax.ShapeDtypeStruct((1, 2048), F32),
        ),
        in_specs=[SMEM, SMEM, VMEM, VMEM],
        out_specs=(VMEM,) * 6,
        scratch_shapes=[
            pltpu.SMEM((32,), jnp.int32),
            pltpu.VMEM((HEAD_DIM, 4096), BF16),
            pltpu.VMEM((2048, HEAD_DIM), F32),
        ],
        compiler_params=PARAMS,
    )(scalars, slope, own, other)


def attend_back_kernel(
    scalar_ref, slope_ref, grad_ref, q_ref, k_ref, v_ref, exact_ref, log_ref,
    dq_out, own_out, other_out,
    sorted_ref, kt_ref, do_ref, dq_ref, dk_ref, dv_ref,
):
    sort_queries(scalar_ref, sorted_ref)
    for source in range(16):
        for half in range(2):
            do_ref[run_rows(scalar_ref[source * 2 + half]), :] = grad_ref[
                source, :, pl.ds(half * HEAD_DIM, HEAD_DIM)
            ]
    for chunk in range(4096 // K_TILE):
        rows = pl.ds(chunk * K_TILE, K_TILE)
        kt_ref[:, rows] = k_ref[rows, :].T
    dk_ref[...] = jnp.zeros_like(dk_ref)
    dv_ref[...] = jnp.zeros_like(dv_ref)
    slope = slope_ref[0]
    ramp = lax.broadcasted_iota(jnp.int32, (K_TILE, Q_TILE), 0)
    bias = ramp.astype(F32) * slope

    def tile_step(tile, unused):
        q_rows = pl.ds(pl.multiple_of(tile * Q_TILE, Q_TILE), Q_TILE)
        query = q_ref[q_rows, :]
        d_out = do_ref[q_rows, :]
        places = query_places(sorted_ref, tile)
        full, every = chunk_bounds(sorted_ref, tile)
        log_rows = log_ref[:, q_rows]
        delta = jnp.sum(d_out.astype(F32).T * exact_ref[:, q_rows], axis=0, keepdims=True)

        def chunk_step(masked, chunk, dq):
            k_rows = pl.ds(pl.multiple_of(chunk * K_TILE, K_TILE), K_TILE)
            scores = dot(k_ref[k_rows, :], query, 1, 1) + bias
            offset = slope * (chunk * K_TILE).astype(F32)
            if masked:
                scores = jnp.where(ramp <= places - chunk * K_TILE, scores, NEGATIVE)
            weights = jnp.exp(scores - (log_rows - offset))
            d_weights = dot(v_ref[k_rows, :], d_out, 1, 1)
            d_scores = (weights * (d_weights - delta)).astype(BF16)
            dv_ref[k_rows, :] += dot(weights.astype(BF16), d_out, 1, 0)
            dk_ref[k_rows, :] += dot(d_scores, query, 1, 0)
            return dq + dot(kt_ref[:, k_rows], d_scores, 1, 0)

        dq = jnp.zeros((HEAD_DIM, Q_TILE), F32)
        dq = lax.fori_loop(0, full, functools.partial(chunk_step, False), dq)
        dq = lax.fori_loop(full, every, functools.partial(chunk_step, True), dq)
        dq_ref[q_rows, :] = (dq * HEAD_DIM ** (-0.5)).T
        return unused

    lax.fori_loop(0, 2048 // Q_TILE, tile_step, 0)
    for source in range(16):
        dq_out[source] = jnp.concatenate(
            [dq_ref[run_rows(scalar_ref[source * 2 + half]), :] for half in range(2)], axis=1
        ).astype(BF16)
        for base, target in ((32, own_out), (64, other_out)):
            parts = []
            for half in range(2):
                place = run_rows(scalar_ref[base + source * 2 + half])
                parts += [dk_ref[place, :], dv_ref[place, :]]
            target[source] = jnp.concatenate(parts, axis=1).astype(target.dtype)


def attend_back(scalars, slope, grad, q, k, v, exact, logs):
    return pl.pallas_call(
        attend_back_kernel,
        out_shape=(
            jax.ShapeDtypeStruct((16, RUN, 128), BF16),
            jax.ShapeDtypeStruct((16, RUN, 256), F32),
            jax.ShapeDtypeStruct((16, RUN, 256), BF16),
        ),
        in_specs=[SMEM, SMEM] + [VMEM] * 6,
        out_specs=(VMEM,) * 3,
        scratch_shapes=[
            pltpu.SMEM((32,), jnp.int32),
            pltpu.VMEM((HEAD_DIM, 4096), BF16),
            pltpu.VMEM((2048, HEAD_DIM), BF16),
            pltpu.VMEM((2048, HEAD_DIM), F32),
            pltpu.VMEM((4096, HEAD_DIM), F32),
            pltpu.VMEM((4096, HEAD_DIM), F32),
        ],
        compiler_params=PARAMS,
    )(scalars, slope, grad, q, k, v, exact, logs)


PLANES = [[2 * i + z for i in range(16)] for z in range(2)]


def swap(value, slot):
    return lax.ppermute(value, "wsh", [(i, i ^ slot) for i in range(4)])


def gather_slots(value):
    return jnp.stack([value] + [swap(value, slot) for slot in (1, 2, 3)])


def reduce_slots(partial):
    rows = partial.reshape(4, 128, -1)
    total = rows[0]
    for slot in (1, 2, 3):
        total = total + swap(rows[slot].astype(BF16), slot).astype(F32)
    return total


def in_order(slots, rank):
    return [
        lax.dynamic_index_in_dim(slots, jnp.bitwise_xor(rank, i), 0, keepdims=False)
        for i in range(4)
    ]


def head_exchange(value):
    return lax.all_to_all(value, "ctx", 0, 0, axis_index_groups=PLANES, tiled=True)


def partner(value):
    return lax.ppermute(value, "ctx", [(i, i ^ 1) for i in range(32)])


def sum_pieces(pieces):
    received = lax.all_to_all(pieces, "ctx", 0, 0, tiled=True)
    return jnp.sum(received.astype(F32), axis=0)


def body(
    tokens,
    places,
    w_qkv,
    b_qv,
    w_out,
    b_out,
    norm1_gain,
    norm1_shift,
    norm2_gain,
    norm2_shift,
    w_up,
    b_up,
    w_down,
    b_down,
    cotangent,
):
    rank = lax.axis_index("wsh")
    column = lax.axis_index("ctx")
    plane = column % 2
    head = rank * 4 + (column // 2) % 4

    runs = places[0].reshape(2, RUN)[:, 0] // RUN
    small = jnp.concatenate(
        [
            b_qv, b_out, norm1_gain, norm1_shift, norm2_gain, norm2_shift, b_up, b_down,
            runs.astype(BF16), jnp.zeros((126,), BF16),
        ]
    )
    small = lax.all_gather(small, "wsh", axis=0).astype(F32)
    full_bqv = small[:, 0:512].reshape(-1)
    full_bout = small[:, 512:768].reshape(-1)
    gain_one = small[:, 768:1024].reshape(-1)
    shift_one = small[:, 1024:1280].reshape(-1)
    gain_two = small[:, 1280:1536].reshape(-1)
    shift_two = small[:, 1536:1792].reshape(-1)
    bias_up = lax.dynamic_index_in_dim(small[:, 1792:2816], rank, 0)
    full_bdown = small[:, 2816:3072].reshape(-1)
    slot_runs = jnp.stack(in_order(small[:, 3072:3074], rank))
    runs_out = jnp.broadcast_to(slot_runs[:, None, None, :], (4, 4, 2, 2)).reshape(32, 1, 2)
    runs_out = jnp.pad(jnp.broadcast_to(runs_out, (32, 8, 2)), ((0, 0), (0, 0), (0, 126)))
    all_runs = lax.all_to_all(runs_out, "ctx", 0, 0, tiled=True)[:, 0, :2].astype(jnp.int32)
    all_runs = all_runs.reshape(16, 2, 2)
    own_runs = lax.dynamic_index_in_dim(all_runs, plane, 1, keepdims=False).reshape(32)
    other_runs = lax.dynamic_index_in_dim(all_runs, 1 - plane, 1, keepdims=False).reshape(32)
    ranks = jnp.sum((own_runs[None, :] < own_runs[:, None]).astype(jnp.int32), axis=1)
    scalars = jnp.concatenate([ranks, own_runs, other_runs])
    slope = (
        8.0 * jnp.exp2(-4.0 * (head.astype(F32) + 1.0) / HEADS) / 4096.0
    ).reshape(1)

    token_slots = gather_slots(tokens[0])
    qkv_cols = w_qkv.reshape(256, 3, 4, 256)
    pieces = []
    for slot in range(4):
        piece = lax.dynamic_index_in_dim(
            qkv_cols, jnp.bitwise_xor(rank, slot), 2, keepdims=False
        ).reshape(256, 768)
        pieces.append(swap(piece, slot) if slot else piece)
    part_qkv = jnp.concatenate(in_order(jnp.stack(pieces), rank), axis=0)
    pieces = []
    for slot in range(4):
        piece = lax.dynamic_slice_in_dim(w_up, jnp.bitwise_xor(rank, slot) * 1024, 1024, 1)
        pieces.append(swap(piece, slot) if slot else piece)
    part_up = jnp.concatenate(in_order(jnp.stack(pieces), rank), axis=0)
    d_down = gather_slots(cotangent[0]).reshape(512, 1024)

    normed_one = layer_norm(token_slots.astype(F32), gain_one, shift_one)
    normed_one = normed_one.astype(BF16).reshape(512, 1024)
    mixed = dot(normed_one, part_qkv, 1, 0)
    bias_qkv = jnp.concatenate(
        [
            lax.dynamic_slice_in_dim(full_bqv, rank * 256, 256),
            jnp.zeros((256,), F32),
            lax.dynamic_slice_in_dim(full_bqv, 1024 + rank * 256, 256),
        ]
    ).reshape(1, 768)
    own = head_exchange(pack_qkv(mixed, bias_qkv))
    other = partner(own[:, :, 128:])
    out_packed, q, k, v, exact, logs = attend(scalars, slope, own, other)
    attended = unpack_heads(head_exchange(out_packed))

    residual_in = tokens[0].astype(F32)
    middle = residual_in + reduce_slots(dot(attended, w_out, 1, 0)) + full_bout
    normed_two, norm_two_back = jax.vjp(layer_norm, middle, gain_two, shift_two)
    normed_two = gather_slots(normed_two.astype(BF16)).reshape(512, 1024)
    pre_act = dot(normed_two, part_up, 1, 0) + bias_up
    hidden, gelu_back = jax.vjp(gelu_tanh, pre_act)
    hidden = hidden.astype(BF16)
    output = middle + reduce_slots(dot(hidden, w_down, 1, 0)) + full_bdown

    (d_pre,) = gelu_back(dot(d_down, w_down, 1, 1))
    d_pre = d_pre.astype(BF16)
    d_normed_two = reduce_slots(dot(d_pre, part_up, 1, 1))
    d_norm_two, grad_gain_two, grad_shift_two = norm_two_back(d_normed_two)
    d_output = cotangent[0].astype(F32)
    d_middle = d_output + d_norm_two
    d_branch_own = d_middle.astype(BF16)
    d_branch = gather_slots(d_branch_own).reshape(512, 1024)
    d_attended = dot(d_branch, w_out, 1, 1)

    grad = head_exchange(pack_heads(d_attended))
    dq, dkv_own, dkv_other = attend_back(scalars, slope, grad, q, k, v, exact, logs)
    dkv = (dkv_own + partner(dkv_other).astype(F32)).astype(BF16)
    d_mixed = unpack_qkv(head_exchange(jnp.concatenate([dq, dkv], axis=2)))
    d_normed_one = reduce_slots(dot(d_mixed, part_qkv, 1, 1))
    _, norm_one_back = jax.vjp(layer_norm, residual_in, gain_one, shift_one)
    d_norm_one, grad_gain_one, grad_shift_one = norm_one_back(d_normed_one)
    grad_input = d_middle + d_norm_one

    def row_pieces(grad):
        slots = jnp.stack(in_order(grad.astype(BF16).reshape(4, 32, 8, -1), rank), axis=1)
        return slots.reshape(32, 32, -1)

    def to_owners(pieces, parts):
        slots = pieces.astype(BF16).reshape(4, 8, -1)
        slots = jnp.stack([slots[0]] + [swap(slots[s], s) for s in (1, 2, 3)])
        columns = jnp.stack(in_order(slots, rank)).reshape(4, 8, parts, -1)
        return columns.transpose(2, 1, 0, 3).reshape(parts * 8, -1)

    grad_wdown = dot(hidden, d_down, 0, 0)
    grad_wup = dot(normed_two, d_pre, 0, 0)
    grad_wout = dot(attended, d_branch, 0, 0)
    early = jnp.concatenate(
        [
            grad_wdown.astype(BF16).reshape(32, 32, 1024),
            row_pieces(grad_wup),
            grad_wout.astype(BF16).reshape(32, 8, 1024),
        ],
        axis=1,
    )
    early = sum_pieces(early)
    up_rows = to_owners(early[32:64], 1).reshape(8, 4, 1024).transpose(1, 0, 2).reshape(32, 1024)
    early = jnp.concatenate([early[:32].astype(BF16), up_rows, early[64:].astype(BF16)], axis=0)
    early = lax.all_gather(early, "ctx", axis=0)

    grad_wqkv = dot(normed_one, d_mixed, 0, 0)
    sums = jnp.sum(d_mixed.astype(F32), axis=0)
    grad_bqv = jnp.zeros((2048,), F32)
    grad_bqv = lax.dynamic_update_slice_in_dim(grad_bqv, sums[:256], rank * 256, 0)
    grad_bqv = lax.dynamic_update_slice_in_dim(grad_bqv, sums[512:], 1024 + rank * 256, 0)
    grad_bup = lax.dynamic_update_slice_in_dim(
        jnp.zeros((4, 1024), F32), jnp.sum(d_pre.astype(F32), axis=0)[None], rank, 0
    )
    vectors = jnp.concatenate(
        [
            grad_bqv.reshape(4, 512),
            jnp.sum(d_branch_own.astype(F32), axis=0).reshape(4, 256),
            grad_gain_one.reshape(4, 256),
            grad_shift_one.reshape(4, 256),
            grad_gain_two.reshape(4, 256),
            grad_shift_two.reshape(4, 256),
            grad_bup,
            jnp.sum(d_output, axis=0).reshape(4, 256),
        ],
        axis=1,
    )
    vectors = jnp.stack(in_order(vectors, rank)).reshape(4, 32, 96).transpose(1, 0, 2)
    vectors = jnp.pad(vectors, ((0, 0), (0, 4), (0, 672)))
    late = jnp.concatenate([row_pieces(grad_wqkv), vectors.astype(BF16)], axis=1)
    late = sum_pieces(late)
    mine = late[32:36, :128].astype(BF16)
    vector = mine[0].astype(F32)
    for slot in (1, 2, 3):
        vector = vector + swap(mine[slot], slot).astype(F32)
    vector = jnp.pad(vector.astype(BF16).reshape(1, 128), ((0, 7), (0, 896)))
    late = jnp.concatenate([to_owners(late[:32], 3).reshape(24, 1024), vector], axis=0)
    late = lax.all_gather(late, "ctx", axis=0)

    out_wdown = early[:, :32].astype(F32).reshape(1024, 1024)
    out_wup = early[:, 32:64].astype(F32).reshape(32, 4, 8, 1024)
    out_wup = out_wup.transpose(0, 2, 1, 3).reshape(256, 4096)
    out_wout = early[:, 64:].astype(F32).reshape(256, 1024)
    out_wqkv = late[:, :24].astype(F32).reshape(32, 3, 8, 1024)
    out_wqkv = out_wqkv.transpose(0, 2, 1, 3).reshape(256, 3072)
    out_vec = late[:, 24, :96].astype(F32).reshape(3072)
    return (
        output.astype(BF16)[None],
        grad_input.astype(BF16)[None],
        out_wqkv,
        out_vec[0:512],
        out_wout,
        out_vec[512:768],
        out_vec[768:1024],
        out_vec[1024:1280],
        out_vec[1280:1536],
        out_vec[1536:1792],
        out_wup,
        out_vec[1792:2816],
        out_wdown,
        out_vec[2816:3072],
    )


def solution(mesh):
    rows = P("wsh", "ctx", None)
    matrix = P("wsh", None)
    vector = P("wsh")
    return jax.shard_map(
        body,
        mesh=mesh,
        in_specs=(
            rows, P("wsh", "ctx"), matrix, vector, matrix, vector, vector, vector, vector, vector,
            matrix, vector, matrix, vector, rows,
        ),
        out_specs=(
            rows, rows, matrix, vector, matrix, vector, vector, vector, vector, vector,
            matrix, vector, matrix, vector,
        ),
        check_vma=False,
    )
```

```python
import functools

import jax
import jax.numpy as jnp
import ml_dtypes
import numpy as np
from jax import lax
from jax.experimental import pallas as pl
from jax.experimental.pallas import tpu as pltpu
from jax.sharding import PartitionSpec as P

HEADS = 16
HEAD_DIM = 64
EPS = 1e-05
NEGATIVE = -1e30
RUN = 64
Q_TILE = 256
K_TILE = 512
F32 = jnp.float32
BF16 = jnp.bfloat16
VMEM = pl.BlockSpec(memory_space=pltpu.VMEM)
SMEM = pl.BlockSpec(memory_space=pltpu.SMEM)
PARAMS = pltpu.CompilerParams(vmem_limit_bytes=48 * 1024 * 1024)


def layer_norm(values, gain_vec, shift_vec):
    average = jnp.mean(values, axis=-1, keepdims=True)
    centred = values - average
    variance = jnp.mean(centred * centred, axis=-1, keepdims=True)
    return centred * lax.rsqrt(variance + EPS) * gain_vec + shift_vec


def gelu_tanh(values):
    return (
        0.5
        * values
        * (1.0 + jnp.tanh(0.7978845608028654 * (values + 0.044715 * values * values * values)))
    )


def dot(left, right, left_dim, right_dim):
    return lax.dot_general(
        left, right, (((left_dim,), (right_dim,)), ((), ())), preferred_element_type=F32
    )


VECTORS = (
    (0, 4, 0), (4, 2, 2048), (6, 2, 3072), (8, 2, 4096), (10, 2, 5120), (12, 2, 6144),
    (14, 8, 7168), (22, 2, 11264),
)
MESSAGE_ROWS = RUN + 16


def start_kernel(rank_ref, *refs):
    tokens, (w0, w1, w2a, w2b, w3a, w3b), smalls = refs[:4], refs[4:10], refs[10:14]
    out_ref, normed_ref, weight_ref, vector_ref = refs[14:]
    rank = rank_ref[0]
    for slot, parts in enumerate(((w0,), (w1,), (w2a, w2b), (w3a, w3b))):
        owner = jnp.bitwise_xor(rank, slot)
        size = 256 // len(parts)
        small = smalls[slot][...].astype(F32)
        for i, part in enumerate(parts):
            rows = pl.ds(pl.multiple_of(owner * 256 + i * size, size), size)
            weight_ref[rows, :] = part[...]
        for row, count, base in VECTORS:
            for i in range(count):
                at = pl.multiple_of(base + (owner * count + i) * 128, 128)
                vector_ref[:, pl.ds(at, 128)] = small[row + i : row + i + 1, :]
    gain, shift = vector_ref[:, 3072:4096], vector_ref[:, 4096:5120]
    at = pl.multiple_of(rank * 256, 256)
    biases = (
        vector_ref[:, pl.ds(at, 256)],
        jnp.zeros((1, 256), F32),
        vector_ref[:, pl.ds(pl.multiple_of(1024 + rank * 256, 256), 256)],
    )
    lane = lax.broadcasted_iota(jnp.int32, (16, 384), 1)
    for slot in range(4):
        rows = pl.ds(slot * 128, 128)
        normed = layer_norm(tokens[slot][...].astype(F32), gain, shift).astype(BF16)
        normed_ref[rows, :] = normed
        mixed = dot(normed, weight_ref[...], 1, 0)
        mixed = [mixed[:, part * 256 : part * 256 + 256] + biases[part] for part in range(3)]
        runs = smalls[slot][...].astype(F32)[24:25, :]
        runs = jnp.where(lane % 2 == 0, runs[:, 0:1], runs[:, 1:2]).astype(BF16)
        for head in range(4):
            cols = slice(head * HEAD_DIM, (head + 1) * HEAD_DIM)
            qe, ke, ve = (part[:RUN, cols] for part in mixed)
            ql, kl, vl = (part[RUN:, cols] for part in mixed)
            message = jnp.concatenate([qe, ql, ke, ve, kl, vl], axis=1).astype(BF16)
            out_ref[slot * 4 + head, :RUN, :] = message
            out_ref[slot * 4 + head, RUN:, :] = runs


def start(rank, tokens, weights, smalls):
    args = (rank, *tokens, *weights, *smalls)
    return pl.pallas_call(
        start_kernel,
        out_shape=(
            jax.ShapeDtypeStruct((16, MESSAGE_ROWS, 384), BF16),
            jax.ShapeDtypeStruct((512, 1024), BF16),
            jax.ShapeDtypeStruct((1024, 768), BF16),
            jax.ShapeDtypeStruct((1, 12288), F32),
        ),
        in_specs=[SMEM] + [VMEM] * (len(args) - 1),
        out_specs=(VMEM,) * 4,
        compiler_params=PARAMS,
    )(*args)


def pack_heads_kernel(flat_ref, out_ref):
    for slot in range(4):
        for head in range(4):
            cols = pl.ds(head * HEAD_DIM, HEAD_DIM)
            out_ref[slot * 4 + head] = jnp.concatenate(
                [
                    flat_ref[pl.ds(slot * 128, RUN), cols],
                    flat_ref[pl.ds(slot * 128 + RUN, RUN), cols],
                ],
                axis=1,
            ).astype(BF16)


def pack_heads(flat):
    return pl.pallas_call(
        pack_heads_kernel,
        out_shape=jax.ShapeDtypeStruct((16, RUN, 128), BF16),
        in_specs=[VMEM],
        out_specs=VMEM,
        compiler_params=PARAMS,
    )(flat)


def unpack_heads_kernel(packed_ref, out_ref):
    for slot in range(4):
        for half in range(2):
            rows = pl.ds(slot * 128 + half * RUN, RUN)
            out_ref[rows, :] = jnp.concatenate(
                [
                    packed_ref[slot * 4 + head, :, pl.ds(half * HEAD_DIM, HEAD_DIM)]
                    for head in range(4)
                ],
                axis=1,
            )


def unpack_heads(packed):
    return pl.pallas_call(
        unpack_heads_kernel,
        out_shape=jax.ShapeDtypeStruct((512, 256), BF16),
        in_specs=[VMEM],
        out_specs=VMEM,
        compiler_params=PARAMS,
    )(packed)


def unpack_qkv_kernel(packed_ref, out_ref):
    starts = ((0, 128, 192), (64, 256, 320))
    for slot in range(4):
        for half in range(2):
            rows = pl.ds(slot * 128 + half * RUN, RUN)
            out_ref[rows, :] = jnp.concatenate(
                [
                    packed_ref[slot * 4 + head, :, pl.ds(starts[half][part], HEAD_DIM)]
                    for part in range(3)
                    for head in range(4)
                ],
                axis=1,
            )


def unpack_qkv(packed):
    return pl.pallas_call(
        unpack_qkv_kernel,
        out_shape=jax.ShapeDtypeStruct((512, 768), BF16),
        in_specs=[VMEM],
        out_specs=VMEM,
        compiler_params=PARAMS,
    )(packed)


HALF_ROWS = 2048
RANK, ORDER, SORTED = 0, 40, 80
SLOPES = (8.0 * 2.0 ** (-4.0 * (np.arange(HEADS) + 1.0) / HEADS) / 4096.0).astype(np.float32)


def slope_table():
    rest, parts = SLOPES, []
    for _ in range(3):
        parts.append(rest.astype(ml_dtypes.bfloat16).astype(np.float32))
        rest = rest - parts[-1]
    return np.stack(parts, axis=1).reshape(-1)


def sort_runs(runs_ref, sorted_ref, place_ref):
    for place in range(64):
        place_ref[place] = 32
    for source in range(32):
        place_ref[runs_ref[source]] = source

    def step(place, count):
        source = place_ref[place]
        sorted_ref[RANK + source] = count
        sorted_ref[ORDER + count] = place
        return count + (source < 32).astype(jnp.int32)

    lax.fori_loop(0, 64, step, 0)


def run_rows(index):
    return pl.ds(pl.multiple_of(index * RUN, RUN), RUN)


def tile_rows(index, size):
    return pl.ds(pl.multiple_of(index * size, size), size)


def tile_limits(sorted_ref, tile, own):
    per = Q_TILE // RUN
    lane = lax.broadcasted_iota(jnp.int32, (1, Q_TILE), 1)
    if own:
        lowest = tile * Q_TILE
        return lane + lowest, (lowest + 1) // K_TILE, (lowest + Q_TILE - 1) // K_TILE + 1
    counts = [
        (sorted_ref[ORDER + tile * per + i] - (tile * per + i)) * RUN for i in range(per)
    ]
    limits = jnp.zeros((1, Q_TILE), jnp.int32)
    for i in range(per):
        limits = jnp.where(lane // RUN == i, counts[i] - 1, limits)
    return limits, counts[0] // K_TILE, (counts[per - 1] + K_TILE - 1) // K_TILE


def slope_lanes(head_ref, slope_ref):
    lane = lax.broadcasted_iota(jnp.int32, (RUN, HEAD_DIM), 1)
    lanes = jnp.zeros((RUN, HEAD_DIM), F32)
    for i in range(3):
        slope = slope_ref[head_ref[0] * 3 + i]
        lanes = jnp.where(lane == i, slope * RUN, lanes)
        lanes = jnp.where(lane == 3 + i, slope, lanes)
    return lanes.astype(BF16)


def sort_keys(runs_ref, sorted_ref, packed_ref, first_lane, k_ref, v_ref):
    lane = lax.broadcasted_iota(jnp.int32, (RUN, HEAD_DIM), 1)
    offset = lax.broadcasted_iota(jnp.int32, (RUN, HEAD_DIM), 0)
    for source in range(16):
        for half in range(2):
            index = source * 2 + half
            place = run_rows(sorted_ref[RANK + index])
            lanes = jnp.where(lane < 3, runs_ref[index], offset)
            lanes = jnp.where(lane < 6, lanes, 0).astype(F32).astype(BF16)
            at = first_lane + half * 128
            k_ref[place, :] = jnp.concatenate(
                [packed_ref[source, :RUN, pl.ds(at, HEAD_DIM)], lanes], axis=1
            )
            v_ref[place, :] = packed_ref[source, :RUN, pl.ds(at + HEAD_DIM, HEAD_DIM)]


def transpose_rows(source_ref, target_ref):
    for chunk in range(HALF_ROWS // K_TILE):
        rows = pl.ds(chunk * K_TILE, K_TILE)
        target_ref[:, rows] = source_ref[rows, :HEAD_DIM].T


def loop_chunks(step, limits, carry):
    _, full, every = limits
    carry = lax.fori_loop(0, full, functools.partial(step, False), carry)
    return lax.fori_loop(full, every, functools.partial(step, True), carry)


def masked_scores(masked, chunk, key, query, limits):
    scores = dot(key, query, 1, 1)
    if masked:
        ramp = lax.broadcasted_iota(jnp.int32, (K_TILE, Q_TILE), 0)
        scores = jnp.where(ramp <= limits[0] - chunk * K_TILE, scores, NEGATIVE)
    return scores


def fold_tile(query, limits, carry, k_ref, vt_ref):
    def step(masked, chunk, carry):
        highest, total, accum = carry
        k_rows = tile_rows(chunk, K_TILE)
        scores = masked_scores(masked, chunk, k_ref[k_rows, :], query, limits)
        new_high = jnp.maximum(highest, jnp.max(scores, axis=0, keepdims=True))
        weights = jnp.exp(scores - new_high)
        factor = jnp.exp(highest - new_high)
        total = total * factor + jnp.sum(weights, axis=0, keepdims=True)
        accum = accum * factor + dot(vt_ref[:, k_rows], weights.astype(BF16), 1, 0)
        return new_high, total, accum

    return loop_chunks(step, limits, carry)


def attend_own_kernel(
    head_ref, slope_ref, runs_ref, own_ref,
    sorted_ref, q_ref, k_ref, v_ref, high_ref, total_ref, accum_ref,
    place_ref, vt_ref,
):
    sort_runs(runs_ref, sorted_ref, place_ref)
    lanes = slope_lanes(head_ref, slope_ref)
    for source in range(16):
        for half in range(2):
            query = own_ref[source, :RUN, pl.ds(half * HEAD_DIM, HEAD_DIM)].astype(F32)
            q_ref[run_rows(sorted_ref[RANK + source * 2 + half]), :] = jnp.concatenate(
                [(query * HEAD_DIM ** (-0.5)).astype(BF16), lanes], axis=1
            )
    sort_keys(runs_ref, sorted_ref, own_ref, 128, k_ref, v_ref)
    transpose_rows(v_ref, vt_ref)

    def tile_step(tile, unused):
        q_rows = tile_rows(tile, Q_TILE)
        carry = (
            jnp.full((1, Q_TILE), NEGATIVE, F32),
            jnp.zeros((1, Q_TILE), F32),
            jnp.zeros((HEAD_DIM, Q_TILE), F32),
        )
        limits = tile_limits(sorted_ref, tile, True)
        carry = fold_tile(q_ref[q_rows, :], limits, carry, k_ref, vt_ref)
        high_ref[:, q_rows], total_ref[:, q_rows], accum_ref[:, q_rows] = carry
        return unused

    lax.fori_loop(0, HALF_ROWS // Q_TILE, tile_step, 0)


def attend_other_kernel(
    own_sorted_ref, runs_ref, other_ref, q_ref, high_ref, total_ref, accum_ref,
    out_ref, sorted_ref, k_ref, v_ref, exact_ref, log_ref,
    place_ref, vt_ref, rows_ref,
):
    sort_runs(runs_ref, sorted_ref, place_ref)
    sort_keys(runs_ref, sorted_ref, other_ref, 0, k_ref, v_ref)
    transpose_rows(v_ref, vt_ref)

    def tile_step(tile, unused):
        q_rows = tile_rows(tile, Q_TILE)
        carry = (high_ref[:, q_rows], total_ref[:, q_rows], accum_ref[:, q_rows])
        limits = tile_limits(own_sorted_ref, tile, False)
        highest, total, accum = fold_tile(q_ref[q_rows, :], limits, carry, k_ref, vt_ref)
        exact = accum / total
        exact_ref[:, q_rows] = exact
        log_ref[:, q_rows] = highest + jnp.log(total)
        rows_ref[q_rows, :] = exact.T
        return unused

    lax.fori_loop(0, HALF_ROWS // Q_TILE, tile_step, 0)
    for source in range(16):
        out_ref[source] = jnp.concatenate(
            [rows_ref[run_rows(own_sorted_ref[RANK + source * 2 + half]), :] for half in range(2)],
            axis=1,
        ).astype(BF16)


def unfold_tile(query, d_out, logs, delta, limits, dq, k_ref, v_ref, kt_ref, dk_ref, dv_ref):
    def step(masked, chunk, dq):
        k_rows = tile_rows(chunk, K_TILE)
        scores = masked_scores(masked, chunk, k_ref[k_rows, :], query, limits)
        weights = jnp.exp(scores - logs)
        d_weights = dot(v_ref[k_rows, :], d_out, 1, 1)
        d_scores = (weights * (d_weights - delta)).astype(BF16)
        dv_ref[k_rows, :] += dot(weights.astype(BF16), d_out, 1, 0)
        dk_ref[k_rows, :] += dot(d_scores, query, 1, 0)
        return dq + dot(kt_ref[:, k_rows], d_scores, 1, 0)

    return loop_chunks(step, limits, dq)


def write_keys(sorted_ref, dk_ref, dv_ref, target):
    for source in range(16):
        parts = []
        for half in range(2):
            place = run_rows(sorted_ref[RANK + source * 2 + half])
            parts += [dk_ref[place, :HEAD_DIM], dv_ref[place, :]]
        target[source] = jnp.concatenate(parts, axis=1).astype(target.dtype)


def back_other_kernel(
    own_sorted_ref, sorted_ref, grad_ref, q_ref, k_ref, v_ref, exact_ref, log_ref,
    other_out, dq_ref, do_ref, delta_ref,
    kt_ref, dk_ref, dv_ref,
):
    for source in range(16):
        for half in range(2):
            do_ref[run_rows(own_sorted_ref[RANK + source * 2 + half]), :] = grad_ref[
                source, :, pl.ds(half * HEAD_DIM, HEAD_DIM)
            ]
    transpose_rows(k_ref, kt_ref)
    dk_ref[...] = jnp.zeros_like(dk_ref)
    dv_ref[...] = jnp.zeros_like(dv_ref)

    def tile_step(tile, unused):
        q_rows = tile_rows(tile, Q_TILE)
        d_out = do_ref[q_rows, :]
        delta = jnp.sum(d_out.astype(F32).T * exact_ref[:, q_rows], axis=0, keepdims=True)
        delta_ref[:, q_rows] = delta
        dq_ref[:, q_rows] = unfold_tile(
            q_ref[q_rows, :], d_out, log_ref[:, q_rows], delta,
            tile_limits(own_sorted_ref, tile, False), jnp.zeros((HEAD_DIM, Q_TILE), F32),
            k_ref, v_ref, kt_ref, dk_ref, dv_ref,
        )
        return unused

    lax.fori_loop(0, HALF_ROWS // Q_TILE, tile_step, 0)
    write_keys(sorted_ref, dk_ref, dv_ref, other_out)


def back_own_kernel(
    sorted_ref, do_ref, q_ref, k_ref, v_ref, delta_ref, log_ref, dq_ref,
    dq_out, own_out,
    kt_ref, rows_ref, dk_ref, dv_ref,
):
    transpose_rows(k_ref, kt_ref)
    dk_ref[...] = jnp.zeros_like(dk_ref)
    dv_ref[...] = jnp.zeros_like(dv_ref)

    def tile_step(tile, unused):
        q_rows = tile_rows(tile, Q_TILE)
        dq = unfold_tile(
            q_ref[q_rows, :], do_ref[q_rows, :], log_ref[:, q_rows], delta_ref[:, q_rows],
            tile_limits(sorted_ref, tile, True), dq_ref[:, q_rows],
            k_ref, v_ref, kt_ref, dk_ref, dv_ref,
        )
        rows_ref[q_rows, :] = (dq * HEAD_DIM ** (-0.5)).T
        return unused

    lax.fori_loop(0, HALF_ROWS // Q_TILE, tile_step, 0)
    for source in range(16):
        dq_out[source] = jnp.concatenate(
            [rows_ref[run_rows(sorted_ref[RANK + source * 2 + half]), :] for half in range(2)],
            axis=1,
        ).astype(BF16)
    write_keys(sorted_ref, dk_ref, dv_ref, own_out)


def shape(*dims, dtype=F32):
    return jax.ShapeDtypeStruct(dims, dtype)


def call_attention(kernel, args, outs, scratch, smem):
    return pl.pallas_call(
        kernel,
        out_shape=outs,
        in_specs=[SMEM] * smem + [VMEM] * (len(args) - smem),
        out_specs=tuple(SMEM if out.dtype == jnp.int32 else VMEM for out in outs),
        scratch_shapes=scratch,
        compiler_params=PARAMS,
        cost_estimate=pl.CostEstimate(
            flops=12_000_000_000, bytes_accessed=4_000_000, transcendentals=4_000_000
        ),
    )(*args)


Q_SHAPE = shape(HALF_ROWS, 128, dtype=BF16)
V_SHAPE = shape(HALF_ROWS, HEAD_DIM, dtype=BF16)
ROW_SHAPE = shape(1, HALF_ROWS)
COLUMN_SHAPE = shape(HEAD_DIM, HALF_ROWS)
FLIPPED = pltpu.VMEM((HEAD_DIM, HALF_ROWS), BF16)
NARROW = pltpu.VMEM((HALF_ROWS, HEAD_DIM), F32)
WIDE = pltpu.VMEM((HALF_ROWS, 128), F32)


SORTED_SHAPE = shape(SORTED, dtype=jnp.int32)
PLACES = pltpu.SMEM((64,), jnp.int32)


def attend_own(*args):
    outs = (SORTED_SHAPE, Q_SHAPE, Q_SHAPE, V_SHAPE, ROW_SHAPE, ROW_SHAPE, COLUMN_SHAPE)
    return call_attention(attend_own_kernel, args, outs, [PLACES, FLIPPED], 3)


def attend_other(*args):
    outs = (shape(16, RUN, 128, dtype=BF16), SORTED_SHAPE, Q_SHAPE, V_SHAPE, COLUMN_SHAPE, ROW_SHAPE)
    return call_attention(attend_other_kernel, args, outs, [PLACES, FLIPPED, NARROW], 2)


def back_other(*args):
    outs = (shape(16, RUN, 256, dtype=BF16), COLUMN_SHAPE, V_SHAPE, ROW_SHAPE)
    return call_attention(back_other_kernel, args, outs, [FLIPPED, WIDE, NARROW], 2)


def back_own(*args):
    outs = (shape(16, RUN, 128, dtype=BF16), shape(16, RUN, 256))
    return call_attention(back_own_kernel, args, outs, [FLIPPED, NARROW, WIDE, NARROW], 1)


PLANES = [[2 * i + z for i in range(16)] for z in range(2)]


def swap(value, slot):
    return lax.ppermute(value, "wsh", [(i, i ^ slot) for i in range(4)])


def gather_list(value):
    across = swap(value, 2)
    return [value, swap(value, 1), across, swap(across, 1)]


def gather_slots(value):
    return jnp.concatenate(gather_list(value), axis=0)


def swap_weight(piece, slot):
    if slot == 0:
        return [piece]
    if slot == 1:
        return [swap(piece, 1)]
    rows = piece.shape[0] // 2
    wrapped = [(c * 4 + r, (c ^ 1) * 4 + (r ^ slot)) for c in range(32) for r in range(4)]
    return [swap(piece[:rows], slot), lax.ppermute(piece[rows:], ("ctx", "wsh"), wrapped)]


def reduce_slots(partial):
    rows = partial.reshape(4, 128, -1)
    across = rows[2] + swap(rows[3].astype(BF16), 1).astype(F32)
    across = swap(across.astype(BF16), 2).astype(F32)
    return rows[0] + swap(rows[1].astype(BF16), 1).astype(F32) + across


def in_order(slots, rank):
    return [
        lax.dynamic_index_in_dim(slots, jnp.bitwise_xor(rank, i), 0, keepdims=False)
        for i in range(4)
    ]


def head_exchange(value):
    return lax.all_to_all(value, "ctx", 0, 0, axis_index_groups=PLANES, tiled=True)


def partner(value):
    return lax.ppermute(value, "ctx", [(i, i ^ 1) for i in range(32)])


def plane_pieces(pieces):
    return head_exchange(pieces.reshape(16, -1, pieces.shape[2]))


def plane_sum(received):
    total = jnp.sum(received.astype(F32), axis=0).astype(BF16)
    return total.astype(F32) + partner(total).astype(F32)


def plane_gather(shard):
    return lax.all_gather(shard, "ctx", axis=0, axis_index_groups=PLANES)


def spread(shard):
    rows = jnp.broadcast_to(shard, (16,) + shard.shape)
    return head_exchange(rows).reshape(rows.shape)


def body(
    tokens,
    places,
    w_qkv,
    b_qv,
    w_out,
    b_out,
    norm1_gain,
    norm1_shift,
    norm2_gain,
    norm2_shift,
    w_up,
    b_up,
    w_down,
    b_down,
    cotangent,
):
    rank = lax.axis_index("wsh")
    column = lax.axis_index("ctx")
    head = rank * 4 + (column // 2) % 4

    pieces = []
    for slot in range(4):
        first = jnp.bitwise_xor(rank, slot) * 256
        parts = [lax.dynamic_slice_in_dim(w_qkv, part * 1024 + first, 256, 1) for part in range(3)]
        pieces += swap_weight(jnp.concatenate(parts, axis=1), slot)
    vectors = (b_qv, b_out, norm1_gain, norm1_shift, norm2_gain, norm2_shift, b_up, b_down)
    runs = (places[0].reshape(2, RUN)[:, 0] // RUN).astype(BF16)
    small = [item.reshape(-1, 128) for item in vectors]
    small = jnp.concatenate(small + [jnp.pad(runs.reshape(1, 2), ((0, 0), (0, 126)))], axis=0)
    smalls = [small] + [swap(small, slot) for slot in (1, 2, 3)]
    packed, normed_one, part_qkv, vector = start(
        rank.astype(jnp.int32).reshape(1), gather_list(tokens[0]), pieces, smalls
    )
    full_bout = vector[0, 2048:3072]
    gain_one = vector[0, 3072:4096]
    shift_one = vector[0, 4096:5120]
    gain_two = vector[0, 5120:6144]
    shift_two = vector[0, 6144:7168]
    bias_up = lax.dynamic_slice_in_dim(vector, 7168 + rank * 1024, 1024, 1)
    full_bdown = vector[0, 11264:]

    packed, w_up, cotangent = lax.optimization_barrier((packed, w_up, cotangent))
    own = head_exchange(packed)

    up_pieces = []
    for slot in range(4):
        piece = lax.dynamic_slice_in_dim(w_up, jnp.bitwise_xor(rank, slot) * 1024, 1024, 1)
        up_pieces += swap_weight(piece, slot)
    d_down = gather_list(cotangent[0])

    def run_indices(message):
        return message[:, RUN, :2].astype(jnp.int32).reshape(32)

    other = partner(own[:, :, 128:])
    own_sorted, q, k_own, v_own, *state = attend_own(
        head.astype(jnp.int32).reshape(1), slope_table(), run_indices(own), own
    )
    out_packed, other_sorted, k_other, v_other, exact, logs = attend_other(
        own_sorted, run_indices(other), other, q, *state
    )
    out_packed, up_pieces, d_down = lax.optimization_barrier((out_packed, up_pieces, d_down))
    up_slots = [
        up_pieces[0], up_pieces[1],
        jnp.concatenate(up_pieces[2:4], axis=0), jnp.concatenate(up_pieces[4:], axis=0),
    ]
    part_up = jnp.concatenate(in_order(jnp.stack(up_slots), rank), axis=0)
    d_down = jnp.concatenate(d_down, axis=0)
    attended = unpack_heads(head_exchange(out_packed))

    def row_pieces(grad):
        slots = jnp.stack(in_order(grad.astype(BF16).reshape(4, 32, 8, -1), rank), axis=1)
        return slots.reshape(32, 32, -1)

    def to_owners(pieces, parts):
        slots = pieces.astype(BF16).reshape(2, 4, 8, -1).transpose(1, 0, 2, 3)
        slots = jnp.stack([slots[0]] + [swap(slots[s], s) for s in (1, 2, 3)])
        columns = jnp.stack(in_order(slots, rank)).reshape(4, 2, 8, parts, -1)
        return columns.transpose(1, 3, 2, 0, 4).reshape(2, parts, 8, -1)

    residual_in = tokens[0].astype(F32)
    middle = residual_in + reduce_slots(dot(attended, w_out, 1, 0)) + full_bout
    normed_two, norm_two_back = jax.vjp(layer_norm, middle, gain_two, shift_two)
    normed_two = gather_slots(normed_two.astype(BF16))
    pre_act = dot(normed_two, part_up, 1, 0) + bias_up
    hidden, gelu_back = jax.vjp(gelu_tanh, pre_act)
    hidden = hidden.astype(BF16)
    early_wdown = dot(hidden, d_down, 0, 0).astype(BF16).reshape(32, 32, 1024)

    (d_pre,) = gelu_back(dot(d_down, w_down, 1, 1))
    d_pre, early_wdown = lax.optimization_barrier((d_pre.astype(BF16), early_wdown))
    grad_wdown = plane_pieces(early_wdown)
    d_normed_two = reduce_slots(dot(d_pre, part_up, 1, 1))
    d_norm_two, grad_gain_two, grad_shift_two = norm_two_back(d_normed_two)
    d_output = cotangent[0].astype(F32)
    d_middle = d_output + d_norm_two
    d_branch_own = d_middle.astype(BF16)
    d_branch = gather_slots(d_branch_own)
    d_attended = dot(d_branch, w_out, 1, 1)

    d_packed, grad_wdown, hidden = lax.optimization_barrier(
        (pack_heads(d_attended), grad_wdown, hidden)
    )
    grad = head_exchange(d_packed)
    early = jnp.concatenate(
        [
            row_pieces(dot(normed_two, d_pre, 0, 0)),
            dot(attended, d_branch, 0, 0).astype(BF16).reshape(32, 8, 1024),
        ],
        axis=1,
    )
    grad, early, hidden = lax.optimization_barrier((grad, early, hidden))
    early = plane_pieces(early)
    grad_wdown = plane_gather(plane_sum(grad_wdown).astype(BF16))
    output = middle + reduce_slots(dot(hidden, w_down, 1, 0)) + full_bdown
    dkv_other, dq, d_out, delta = back_other(own_sorted, other_sorted, grad, q, k_other, v_other, exact, logs)
    dkv_other = partner(dkv_other)
    dq, dkv_own = back_own(own_sorted, d_out, q, k_own, v_own, delta, logs, dq)
    early, output, dq = lax.optimization_barrier((early, output, dq))
    dkv = (dkv_own + dkv_other.astype(F32)).astype(BF16)
    early = plane_sum(early).reshape(2, 40, 1024)
    up_rows = to_owners(early[:, :32], 1).reshape(2, 8, 4, 1024).transpose(0, 2, 1, 3)
    early = jnp.concatenate(
        [up_rows.reshape(2, 32, 1024), early[:, 32:].astype(BF16)], axis=1
    ).reshape(80, 1024)
    d_packed = head_exchange(jnp.concatenate([dq, dkv], axis=2))
    early, d_packed = lax.optimization_barrier((early, d_packed))
    early = plane_gather(early)
    d_mixed = unpack_qkv(d_packed)
    d_normed_one = reduce_slots(dot(d_mixed, part_qkv, 1, 1))
    _, norm_one_back = jax.vjp(layer_norm, residual_in, gain_one, shift_one)
    d_norm_one, grad_gain_one, grad_shift_one = norm_one_back(d_normed_one)
    grad_input = d_middle + d_norm_one

    grad_wqkv = row_pieces(dot(normed_one, d_mixed, 0, 0))
    late = plane_pieces(grad_wqkv)
    sums = jnp.sum(d_mixed.astype(F32), axis=0)
    grad_bqv = jnp.zeros((2048,), F32)
    grad_bqv = lax.dynamic_update_slice_in_dim(grad_bqv, sums[:256], rank * 256, 0)
    grad_bqv = lax.dynamic_update_slice_in_dim(grad_bqv, sums[512:], 1024 + rank * 256, 0)
    grad_bup = lax.dynamic_update_slice_in_dim(
        jnp.zeros((4, 1024), F32), jnp.sum(d_pre.astype(F32), axis=0)[None], rank, 0
    )
    vectors = jnp.concatenate(
        [
            grad_bqv.reshape(4, 512),
            jnp.sum(d_branch_own.astype(F32), axis=0).reshape(4, 256),
            grad_gain_one.reshape(4, 256),
            grad_shift_one.reshape(4, 256),
            grad_gain_two.reshape(4, 256),
            grad_shift_two.reshape(4, 256),
            grad_bup,
            jnp.sum(d_output, axis=0).reshape(4, 256),
        ],
        axis=1,
    )
    vectors = jnp.stack(in_order(vectors, rank)).reshape(4, 24, 128).astype(BF16)
    vectors = vectors.astype(F32) + partner(vectors).astype(F32)
    vector = vectors[0]
    for slot in (1, 2, 3):
        vector = vector + swap(vectors[slot].astype(BF16), slot).astype(F32)
    late, vector = lax.optimization_barrier((late, vector))
    late = to_owners(plane_sum(late).reshape(2, 32, 768), 3).reshape(2, 3, 8, 8, 128)
    late = late.transpose(0, 1, 3, 2, 4).reshape(384, 128)
    late = spread(jnp.concatenate([late, vector.astype(BF16)], axis=0))

    out_wdown = grad_wdown.astype(F32).reshape(1024, 1024)
    early = early.reshape(32, 40, 1024)
    out_wup = early[:, :32].astype(F32).reshape(32, 4, 8, 1024)
    out_wup = out_wup.transpose(0, 2, 1, 3).reshape(256, 4096)
    out_wout = early[:, 32:].astype(F32).reshape(256, 1024)
    out_wqkv = late[:, :384].reshape(32, 24, 8, 128).astype(F32)
    out_wqkv = out_wqkv.transpose(0, 2, 1, 3).reshape(256, 3072)
    out_vec = jnp.sum(late[:, 384:].astype(F32), axis=0).reshape(3072)
    return (
        output.astype(BF16)[None],
        grad_input.astype(BF16)[None],
        out_wqkv,
        out_vec[0:512],
        out_wout,
        out_vec[512:768],
        out_vec[768:1024],
        out_vec[1024:1280],
        out_vec[1280:1536],
        out_vec[1536:1792],
        out_wup,
        out_vec[1792:2816],
        out_wdown,
        out_vec[2816:3072],
    )


def solution(mesh):
    rows = P("wsh", "ctx", None)
    matrix = P("wsh", None)
    vector = P("wsh")
    return jax.shard_map(
        body,
        mesh=mesh,
        in_specs=(
            rows, P("wsh", "ctx"), matrix, vector, matrix, vector, vector, vector, vector, vector,
            matrix, vector, matrix, vector, rows,
        ),
        out_specs=(
            rows, rows, matrix, vector, matrix, vector, vector, vector, vector, vector,
            matrix, vector, matrix, vector,
        ),
        check_vma=False,
    )
```

```python
import functools

import jax
import jax.numpy as jnp
import ml_dtypes
import numpy as np
from jax import lax
from jax.experimental import pallas as pl
from jax.experimental.pallas import tpu as pltpu
from jax.sharding import PartitionSpec as P

HEADS = 16
HEAD_DIM = 64
EPS = 1e-05
NEGATIVE = -1e30
RUN = 64
Q_TILE = 512
K_TILE = 512
F32 = jnp.float32
BF16 = jnp.bfloat16
VMEM = pl.BlockSpec(memory_space=pltpu.VMEM)
SMEM = pl.BlockSpec(memory_space=pltpu.SMEM)
PARAMS = pltpu.CompilerParams(vmem_limit_bytes=20 * 1024 * 1024)
SMALL = pltpu.CompilerParams(vmem_limit_bytes=8 * 1024 * 1024)


def layer_norm(values, gain_vec, shift_vec):
    average = jnp.mean(values, axis=-1, keepdims=True)
    centred = values - average
    variance = jnp.mean(centred * centred, axis=-1, keepdims=True)
    return centred * lax.rsqrt(variance + EPS) * gain_vec + shift_vec


def gelu_tanh(values):
    return (
        0.5
        * values
        * (1.0 + jnp.tanh(0.7978845608028654 * (values + 0.044715 * values * values * values)))
    )


def dot(left, right, left_dim, right_dim):
    return lax.dot_general(
        left, right, (((left_dim,), (right_dim,)), ((), ())), preferred_element_type=F32
    )


VECTORS = (
    (0, 4, 0), (4, 2, 2048), (6, 2, 3072), (8, 2, 4096), (10, 2, 5120), (12, 2, 6144),
    (14, 8, 7168), (22, 2, 11264),
)
MESSAGE_ROWS = RUN + 16


def start_kernel(rank_ref, *refs):
    tokens, (w0, w1, w2a, w2b, w3a, w3b), smalls = refs[:4], refs[4:10], refs[10:14]
    out_ref, normed_ref, weight_ref, vector_ref = refs[14:]
    rank = rank_ref[0]
    for slot, parts in enumerate(((w0,), (w1,), (w2a, w2b), (w3a, w3b))):
        owner = jnp.bitwise_xor(rank, slot)
        size = 256 // len(parts)
        small = smalls[slot][...].astype(F32)
        for i, part in enumerate(parts):
            rows = pl.ds(pl.multiple_of(owner * 256 + i * size, size), size)
            weight_ref[rows, :] = part[...]
        for row, count, base in VECTORS:
            for i in range(count):
                at = pl.multiple_of(base + (owner * count + i) * 128, 128)
                vector_ref[:, pl.ds(at, 128)] = small[row + i : row + i + 1, :]
    gain, shift = vector_ref[:, 3072:4096], vector_ref[:, 4096:5120]
    at = pl.multiple_of(rank * 256, 256)
    biases = (
        vector_ref[:, pl.ds(at, 256)],
        jnp.zeros((1, 256), F32),
        vector_ref[:, pl.ds(pl.multiple_of(1024 + rank * 256, 256), 256)],
    )
    lane = lax.broadcasted_iota(jnp.int32, (16, 384), 1)
    for slot in range(4):
        rows = pl.ds(slot * 128, 128)
        normed = layer_norm(tokens[slot][...].astype(F32), gain, shift).astype(BF16)
        normed_ref[rows, :] = normed
        mixed = dot(normed, weight_ref[...], 1, 0)
        mixed = [mixed[:, part * 256 : part * 256 + 256] + biases[part] for part in range(3)]
        runs = smalls[slot][...].astype(F32)[24:25, :]
        runs = jnp.where(lane % 2 == 0, runs[:, 0:1], runs[:, 1:2]).astype(BF16)
        for head in range(4):
            cols = slice(head * HEAD_DIM, (head + 1) * HEAD_DIM)
            qe, ke, ve = (part[:RUN, cols] for part in mixed)
            ql, kl, vl = (part[RUN:, cols] for part in mixed)
            message = jnp.concatenate([qe, ql, ke, ve, kl, vl], axis=1).astype(BF16)
            out_ref[slot * 4 + head, :RUN, :] = message
            out_ref[slot * 4 + head, RUN:, :] = runs


def start(rank, tokens, weights, smalls):
    args = (rank, *tokens, *weights, *smalls)
    return pl.pallas_call(
        start_kernel,
        out_shape=(
            jax.ShapeDtypeStruct((16, MESSAGE_ROWS, 384), BF16),
            jax.ShapeDtypeStruct((512, 1024), BF16),
            jax.ShapeDtypeStruct((1024, 768), BF16),
            jax.ShapeDtypeStruct((1, 12288), F32),
        ),
        in_specs=[SMEM] + [VMEM] * (len(args) - 1),
        out_specs=(VMEM,) * 4,
        compiler_params=PARAMS,
    )(*args)


def pack_heads_kernel(flat_ref, out_ref):
    for slot in range(4):
        for head in range(4):
            cols = pl.ds(head * HEAD_DIM, HEAD_DIM)
            out_ref[slot * 4 + head] = jnp.concatenate(
                [
                    flat_ref[pl.ds(slot * 128, RUN), cols],
                    flat_ref[pl.ds(slot * 128 + RUN, RUN), cols],
                ],
                axis=1,
            ).astype(BF16)


def pack_heads(flat):
    return pl.pallas_call(
        pack_heads_kernel,
        out_shape=jax.ShapeDtypeStruct((16, RUN, 128), BF16),
        in_specs=[VMEM],
        out_specs=VMEM,
        compiler_params=SMALL,
    )(flat)


def unpack_heads_kernel(packed_ref, out_ref):
    for slot in range(4):
        for half in range(2):
            rows = pl.ds(slot * 128 + half * RUN, RUN)
            out_ref[rows, :] = jnp.concatenate(
                [
                    packed_ref[slot * 4 + head, :, pl.ds(half * HEAD_DIM, HEAD_DIM)]
                    for head in range(4)
                ],
                axis=1,
            )


def unpack_heads(packed):
    return pl.pallas_call(
        unpack_heads_kernel,
        out_shape=jax.ShapeDtypeStruct((512, 256), BF16),
        in_specs=[VMEM],
        out_specs=VMEM,
        compiler_params=SMALL,
    )(packed)


def by_owner(left, right, rank):
    blocks = []
    for slot in range(4):
        at = pl.multiple_of(jnp.bitwise_xor(rank, slot) * 256, 256)
        blocks.append(dot(left[:, pl.ds(at, 256)], right, 0, 0).astype(BF16))
    return blocks


def late_kernel(rank_ref, packed_ref, normed_ref, mixed_ref, out_ref):
    starts = ((0, 128, 192), (64, 256, 320))
    for slot in range(4):
        for half in range(2):
            parts = [[], [], []]
            for head in range(4):
                for part in range(3):
                    lanes = pl.ds(starts[half][part], HEAD_DIM)
                    parts[part].append(packed_ref[slot * 4 + head, :, lanes])
            rows = pl.ds(slot * 128 + half * RUN, RUN)
            mixed_ref[rows, :] = jnp.concatenate(sum(parts, []), axis=1)
    for slot, block in enumerate(by_owner(normed_ref, mixed_ref[...], rank_ref[0])):
        out_ref[:, slot * 16 : slot * 16 + 16, :] = block.reshape(16, 16, 768)


def late_pieces(rank, packed, normed):
    return pl.pallas_call(
        late_kernel,
        out_shape=(
            jax.ShapeDtypeStruct((512, 768), BF16),
            jax.ShapeDtypeStruct((16, 64, 768), BF16),
        ),
        in_specs=[SMEM, VMEM, VMEM],
        out_specs=(VMEM, VMEM),
        compiler_params=PARAMS,
    )(rank, packed, normed)


def early_kernel(
    rank_ref, normed_ref, d_pre_ref, attended_ref, branch_ref, out_ref
):
    for slot, block in enumerate(by_owner(normed_ref, d_pre_ref[...], rank_ref[0])):
        out_ref[:, slot * 16 : slot * 16 + 16, :] = block.reshape(16, 16, 1024)
    block = dot(attended_ref[...], branch_ref[...], 0, 0).astype(BF16)
    out_ref[:, 64:80, :] = block.reshape(16, 16, 1024)


def early_pieces(*args):
    return pl.pallas_call(
        early_kernel,
        out_shape=jax.ShapeDtypeStruct((16, 80, 1024), BF16),
        in_specs=[SMEM] + [VMEM] * 4,
        out_specs=VMEM,
        compiler_params=PARAMS,
    )(*args)


HALF_ROWS = 2048
RANK, ORDER, SORTED = 0, 40, 80
SLOPES = (8.0 * 2.0 ** (-4.0 * (np.arange(HEADS) + 1.0) / HEADS) / 4096.0).astype(np.float32)


def slope_table():
    rest, parts = SLOPES, []
    for _ in range(3):
        parts.append(rest.astype(ml_dtypes.bfloat16).astype(np.float32))
        rest = rest - parts[-1]
    return np.stack(parts, axis=1).reshape(-1)


def sort_runs(runs_ref, sorted_ref, place_ref):
    for place in range(64):
        place_ref[place] = 32
    for source in range(32):
        place_ref[runs_ref[source]] = source

    def step(place, count):
        source = place_ref[place]
        sorted_ref[RANK + source] = count
        sorted_ref[ORDER + count] = place
        return count + (source < 32).astype(jnp.int32)

    lax.fori_loop(0, 64, step, 0)


def run_rows(index):
    return pl.ds(pl.multiple_of(index * RUN, RUN), RUN)


def tile_rows(index, size):
    return pl.ds(pl.multiple_of(index * size, size), size)


def tile_limits(sorted_ref, tile, own):
    per = Q_TILE // RUN
    lane = lax.broadcasted_iota(jnp.int32, (1, Q_TILE), 1)
    if own:
        lowest = tile * Q_TILE
        return lane + lowest, (lowest + 1) // K_TILE, (lowest + Q_TILE - 1) // K_TILE + 1
    counts = [
        (sorted_ref[ORDER + tile * per + i] - (tile * per + i)) * RUN for i in range(per)
    ]
    limits = jnp.zeros((1, Q_TILE), jnp.int32)
    for i in range(per):
        limits = jnp.where(lane // RUN == i, counts[i] - 1, limits)
    return limits, counts[0] // K_TILE, (counts[per - 1] + K_TILE - 1) // K_TILE


def slope_lanes(head_ref, slope_ref):
    lane = lax.broadcasted_iota(jnp.int32, (RUN, HEAD_DIM), 1)
    lanes = jnp.zeros((RUN, HEAD_DIM), F32)
    for i in range(3):
        slope = slope_ref[head_ref[0] * 3 + i]
        lanes = jnp.where(lane == i, slope * RUN, lanes)
        lanes = jnp.where(lane == 3 + i, slope, lanes)
    return lanes.astype(BF16)


def sort_keys(runs_ref, sorted_ref, packed_ref, first_lane, k_ref, v_ref):
    lane = lax.broadcasted_iota(jnp.int32, (RUN, HEAD_DIM), 1)
    offset = lax.broadcasted_iota(jnp.int32, (RUN, HEAD_DIM), 0)
    for source in range(16):
        for half in range(2):
            index = source * 2 + half
            place = run_rows(sorted_ref[RANK + index])
            lanes = jnp.where(lane < 3, runs_ref[index], offset)
            lanes = jnp.where(lane < 6, lanes, 0).astype(F32).astype(BF16)
            at = first_lane + half * 128
            k_ref[place, :] = jnp.concatenate(
                [packed_ref[source, :RUN, pl.ds(at, HEAD_DIM)], lanes], axis=1
            )
            v_ref[place, :] = packed_ref[source, :RUN, pl.ds(at + HEAD_DIM, HEAD_DIM)]


def transpose_rows(source_ref, target_ref):
    for chunk in range(HALF_ROWS // K_TILE):
        rows = pl.ds(chunk * K_TILE, K_TILE)
        target_ref[:, rows] = source_ref[rows, :HEAD_DIM].T


def loop_chunks(step, limits, carry):
    _, full, every = limits
    if isinstance(every, int):
        for chunk in range(every):
            carry = step(chunk >= full, chunk, carry)
        return carry
    carry = lax.fori_loop(0, full, functools.partial(step, False), carry)
    return lax.fori_loop(full, every, functools.partial(step, True), carry)


def masked_scores(masked, chunk, key, query, limits):
    scores = dot(key, query, 1, 1)
    if masked:
        ramp = lax.broadcasted_iota(jnp.int32, (K_TILE, Q_TILE), 0)
        scores = jnp.where(ramp <= limits[0] - chunk * K_TILE, scores, NEGATIVE)
    return scores


def fold_tile(query, limits, carry, k_ref, vt_ref):
    def step(masked, chunk, carry):
        highest, total, accum = carry
        k_rows = tile_rows(chunk, K_TILE)
        scores = masked_scores(masked, chunk, k_ref[k_rows, :], query, limits)
        new_high = jnp.maximum(highest, jnp.max(scores, axis=0, keepdims=True))
        weights = jnp.exp(scores - new_high)
        factor = jnp.exp(highest - new_high)
        total = total * factor + jnp.sum(weights, axis=0, keepdims=True)
        accum = accum * factor + dot(vt_ref[:, k_rows], weights.astype(BF16), 1, 0)
        return new_high, total, accum

    return loop_chunks(step, limits, carry)


def attend_own_kernel(
    head_ref, slope_ref, runs_ref, own_ref,
    sorted_ref, q_ref, k_ref, v_ref, high_ref, total_ref, accum_ref,
    place_ref, vt_ref,
):
    sort_runs(runs_ref, sorted_ref, place_ref)
    lanes = slope_lanes(head_ref, slope_ref)
    for source in range(16):
        for half in range(2):
            query = own_ref[source, :RUN, pl.ds(half * HEAD_DIM, HEAD_DIM)].astype(F32)
            q_ref[run_rows(sorted_ref[RANK + source * 2 + half]), :] = jnp.concatenate(
                [(query * HEAD_DIM ** (-0.5)).astype(BF16), lanes], axis=1
            )
    sort_keys(runs_ref, sorted_ref, own_ref, 128, k_ref, v_ref)
    transpose_rows(v_ref, vt_ref)

    def tile_step(tile, unused):
        q_rows = tile_rows(tile, Q_TILE)
        carry = (
            jnp.full((1, Q_TILE), NEGATIVE, F32),
            jnp.zeros((1, Q_TILE), F32),
            jnp.zeros((HEAD_DIM, Q_TILE), F32),
        )
        limits = tile_limits(sorted_ref, tile, True)
        carry = fold_tile(q_ref[q_rows, :], limits, carry, k_ref, vt_ref)
        high_ref[:, q_rows], total_ref[:, q_rows], accum_ref[:, q_rows] = carry
        return unused

    for tile in range(HALF_ROWS // Q_TILE):
        tile_step(tile, 0)


def attend_other_kernel(
    own_sorted_ref, runs_ref, other_ref, q_ref, high_ref, total_ref, accum_ref,
    out_ref, sorted_ref, k_ref, v_ref, exact_ref, log_ref,
    place_ref, vt_ref, rows_ref,
):
    sort_runs(runs_ref, sorted_ref, place_ref)
    sort_keys(runs_ref, sorted_ref, other_ref, 0, k_ref, v_ref)
    transpose_rows(v_ref, vt_ref)

    def tile_step(tile, unused):
        q_rows = tile_rows(tile, Q_TILE)
        carry = (high_ref[:, q_rows], total_ref[:, q_rows], accum_ref[:, q_rows])
        limits = tile_limits(own_sorted_ref, tile, False)
        highest, total, accum = fold_tile(q_ref[q_rows, :], limits, carry, k_ref, vt_ref)
        exact = accum / total
        exact_ref[:, q_rows] = exact
        log_ref[:, q_rows] = highest + jnp.log(total)
        rows_ref[q_rows, :] = exact.T
        return unused

    lax.fori_loop(0, HALF_ROWS // Q_TILE, tile_step, 0)
    for source in range(16):
        out_ref[source] = jnp.concatenate(
            [rows_ref[run_rows(own_sorted_ref[RANK + source * 2 + half]), :] for half in range(2)],
            axis=1,
        ).astype(BF16)


def unfold_tile(query, d_out, logs, delta, limits, dq, k_ref, v_ref, kt_ref, dk_ref, dv_ref):
    def step(masked, chunk, dq):
        k_rows = tile_rows(chunk, K_TILE)
        scores = masked_scores(masked, chunk, k_ref[k_rows, :], query, limits)
        weights = jnp.exp(scores - logs)
        d_weights = dot(v_ref[k_rows, :], d_out, 1, 1)
        d_scores = (weights * (d_weights - delta)).astype(BF16)
        dv_ref[k_rows, :] += dot(weights.astype(BF16), d_out, 1, 0)
        dk_ref[k_rows, :] += dot(d_scores, query, 1, 0)
        return dq + dot(kt_ref[:, k_rows], d_scores, 1, 0)

    return loop_chunks(step, limits, dq)


def write_keys(sorted_ref, dk_ref, dv_ref, target):
    for source in range(16):
        parts = []
        for half in range(2):
            place = run_rows(sorted_ref[RANK + source * 2 + half])
            parts += [dk_ref[place, :HEAD_DIM], dv_ref[place, :]]
        target[source] = jnp.concatenate(parts, axis=1).astype(target.dtype)


def back_other_kernel(
    own_sorted_ref, sorted_ref, grad_ref, q_ref, k_ref, v_ref, exact_ref, log_ref,
    other_out, dq_ref, do_ref, delta_ref,
    kt_ref, dk_ref, dv_ref,
):
    for source in range(16):
        for half in range(2):
            do_ref[run_rows(own_sorted_ref[RANK + source * 2 + half]), :] = grad_ref[
                source, :, pl.ds(half * HEAD_DIM, HEAD_DIM)
            ]
    transpose_rows(k_ref, kt_ref)
    dk_ref[...] = jnp.zeros_like(dk_ref)
    dv_ref[...] = jnp.zeros_like(dv_ref)

    def tile_step(tile, unused):
        q_rows = tile_rows(tile, Q_TILE)
        d_out = do_ref[q_rows, :]
        delta = jnp.sum(d_out.astype(F32).T * exact_ref[:, q_rows], axis=0, keepdims=True)
        delta_ref[:, q_rows] = delta
        dq_ref[:, q_rows] = unfold_tile(
            q_ref[q_rows, :], d_out, log_ref[:, q_rows], delta,
            tile_limits(own_sorted_ref, tile, False), jnp.zeros((HEAD_DIM, Q_TILE), F32),
            k_ref, v_ref, kt_ref, dk_ref, dv_ref,
        )
        return unused

    lax.fori_loop(0, HALF_ROWS // Q_TILE, tile_step, 0)
    write_keys(sorted_ref, dk_ref, dv_ref, other_out)


def back_own_kernel(
    sorted_ref, do_ref, q_ref, k_ref, v_ref, delta_ref, log_ref, dq_ref,
    dq_out, own_out,
    kt_ref, rows_ref, dk_ref, dv_ref,
):
    transpose_rows(k_ref, kt_ref)
    dk_ref[...] = jnp.zeros_like(dk_ref)
    dv_ref[...] = jnp.zeros_like(dv_ref)

    def tile_step(tile, unused):
        q_rows = tile_rows(tile, Q_TILE)
        dq = unfold_tile(
            q_ref[q_rows, :], do_ref[q_rows, :], log_ref[:, q_rows], delta_ref[:, q_rows],
            tile_limits(sorted_ref, tile, True), dq_ref[:, q_rows],
            k_ref, v_ref, kt_ref, dk_ref, dv_ref,
        )
        rows_ref[q_rows, :] = (dq * HEAD_DIM ** (-0.5)).T
        return unused

    for tile in range(HALF_ROWS // Q_TILE):
        tile_step(tile, 0)
    for source in range(16):
        dq_out[source] = jnp.concatenate(
            [rows_ref[run_rows(sorted_ref[RANK + source * 2 + half]), :] for half in range(2)],
            axis=1,
        ).astype(BF16)
    write_keys(sorted_ref, dk_ref, dv_ref, own_out)


def shape(*dims, dtype=F32):
    return jax.ShapeDtypeStruct(dims, dtype)


def call_attention(kernel, args, outs, scratch, smem):
    return pl.pallas_call(
        kernel,
        out_shape=outs,
        in_specs=[SMEM] * smem + [VMEM] * (len(args) - smem),
        out_specs=tuple(SMEM if out.dtype == jnp.int32 else VMEM for out in outs),
        scratch_shapes=scratch,
        compiler_params=PARAMS,
        cost_estimate=pl.CostEstimate(
            flops=12_000_000_000, bytes_accessed=4_000_000, transcendentals=4_000_000
        ),
    )(*args)


Q_SHAPE = shape(HALF_ROWS, 128, dtype=BF16)
V_SHAPE = shape(HALF_ROWS, HEAD_DIM, dtype=BF16)
ROW_SHAPE = shape(1, HALF_ROWS)
COLUMN_SHAPE = shape(HEAD_DIM, HALF_ROWS)
FLIPPED = pltpu.VMEM((HEAD_DIM, HALF_ROWS), BF16)
NARROW = pltpu.VMEM((HALF_ROWS, HEAD_DIM), F32)
WIDE = pltpu.VMEM((HALF_ROWS, 128), F32)


SORTED_SHAPE = shape(SORTED, dtype=jnp.int32)
PLACES = pltpu.SMEM((64,), jnp.int32)


def attend_own(*args):
    outs = (SORTED_SHAPE, Q_SHAPE, Q_SHAPE, V_SHAPE, ROW_SHAPE, ROW_SHAPE, COLUMN_SHAPE)
    return call_attention(attend_own_kernel, args, outs, [PLACES, FLIPPED], 3)


def attend_other(*args):
    outs = (shape(16, RUN, 128, dtype=BF16), SORTED_SHAPE, Q_SHAPE, V_SHAPE, COLUMN_SHAPE, ROW_SHAPE)
    return call_attention(attend_other_kernel, args, outs, [PLACES, FLIPPED, NARROW], 2)


def back_other(*args):
    outs = (shape(16, RUN, 256, dtype=BF16), COLUMN_SHAPE, V_SHAPE, ROW_SHAPE)
    return call_attention(back_other_kernel, args, outs, [FLIPPED, WIDE, NARROW], 2)


def back_own(*args):
    outs = (shape(16, RUN, 128, dtype=BF16), shape(16, RUN, 256))
    return call_attention(back_own_kernel, args, outs, [FLIPPED, NARROW, WIDE, NARROW], 1)


PLANES = [[2 * i + z for i in range(16)] for z in range(2)]


def swap(value, slot):
    return lax.ppermute(value, "wsh", [(i, i ^ slot) for i in range(4)])


def gather_list(value):
    across = swap(value, 2)
    return [value, swap(value, 1), across, swap(across, 1)]


def gather_slots(value):
    return jnp.concatenate(gather_list(value), axis=0)


def swap_weight(weight, rank, starts, size):
    def columns(slot, row, rows):
        parts = [
            lax.dynamic_slice(
                weight, (row, start + jnp.bitwise_xor(rank, slot) * size), (rows, size)
            )
            for start in starts
        ]
        return jnp.concatenate(parts, axis=1) if len(parts) > 1 else parts[0]

    pieces = [columns(0, 0, 256), columns(1, 0, 256)]
    pieces += [columns(slot, row, 128) for slot in (2, 3) for row in (0, 128)]
    return pieces


def swap_pieces(pieces):
    def wrapped(slot):
        return [(c * 4 + r, (c ^ 1) * 4 + (r ^ slot)) for c in range(32) for r in range(4)]

    return [
        pieces[0], swap(pieces[1], 1),
        swap(pieces[2], 2), lax.ppermute(pieces[3], ("ctx", "wsh"), wrapped(2)),
        swap(pieces[4], 3), lax.ppermute(pieces[5], ("ctx", "wsh"), wrapped(3)),
    ]


def reduce_slots(partial):
    rows = partial.reshape(4, 128, -1)
    across = rows[2] + swap(rows[3].astype(BF16), 1).astype(F32)
    across = swap(across.astype(BF16), 2).astype(F32)
    return rows[0] + swap(rows[1].astype(BF16), 1).astype(F32) + across


def in_order(slots, rank):
    return [
        lax.dynamic_index_in_dim(slots, jnp.bitwise_xor(rank, i), 0, keepdims=False)
        for i in range(4)
    ]


def head_exchange(value):
    return lax.all_to_all(value, "ctx", 0, 0, axis_index_groups=PLANES, tiled=True)


def partner(value):
    return lax.ppermute(value, "ctx", [(i, i ^ 1) for i in range(32)])


def plane_sum(received):
    total = jnp.sum(received.astype(F32), axis=0).astype(BF16)
    return total.astype(F32) + partner(total).astype(F32)


def plane_gather(shard):
    return lax.all_gather(shard, "ctx", axis=0, axis_index_groups=PLANES)


def spread(shard):
    rows = jnp.broadcast_to(shard, (16,) + shard.shape)
    return head_exchange(rows).reshape(rows.shape)


def body(
    tokens,
    places,
    w_qkv,
    b_qv,
    w_out,
    b_out,
    norm1_gain,
    norm1_shift,
    norm2_gain,
    norm2_shift,
    w_up,
    b_up,
    w_down,
    b_down,
    cotangent,
):
    rank = lax.axis_index("wsh")
    column = lax.axis_index("ctx")
    head = rank * 4 + (column // 2) % 4
    rank_scalar = rank.astype(jnp.int32).reshape(1)

    pieces = swap_weight(w_qkv, rank, (0, 1024, 2048), 256)
    vectors = (b_qv, b_out, norm1_gain, norm1_shift, norm2_gain, norm2_shift, b_up, b_down)
    pieces, vectors, places = lax.optimization_barrier((pieces, vectors, places))
    pieces = swap_pieces(pieces)
    runs = (places[0].reshape(2, RUN)[:, 0] // RUN).astype(BF16)
    small = [item.reshape(-1, 128) for item in vectors]
    small = jnp.concatenate(small + [jnp.pad(runs.reshape(1, 2), ((0, 0), (0, 126)))], axis=0)
    smalls = [small] + [swap(small, slot) for slot in (1, 2, 3)]
    smalls, w_up, cotangent = lax.optimization_barrier((smalls, w_up, cotangent))
    packed, normed_one, part_qkv, vector = start(
        rank_scalar, gather_list(tokens[0]), pieces, smalls
    )
    full_bout = vector[0, 2048:3072]
    gain_one = vector[0, 3072:4096]
    shift_one = vector[0, 4096:5120]
    gain_two = vector[0, 5120:6144]
    shift_two = vector[0, 6144:7168]
    bias_up = lax.dynamic_slice_in_dim(vector, 7168 + rank * 1024, 1024, 1)
    full_bdown = vector[0, 11264:]

    own = head_exchange(packed)

    up_pieces = swap_pieces(swap_weight(w_up, rank, (0,), 1024))
    d_down = gather_list(cotangent[0])

    def run_indices(message):
        return message[:, RUN, :2].astype(jnp.int32).reshape(32)

    other = partner(own[:, :, 128:])
    own_sorted, q, k_own, v_own, *state = attend_own(
        head.astype(jnp.int32).reshape(1), slope_table(), run_indices(own), own
    )
    out_packed, other_sorted, k_other, v_other, exact, logs = attend_other(
        own_sorted, run_indices(other), other, q, *state
    )
    out_packed, up_pieces, d_down = lax.optimization_barrier((out_packed, up_pieces, d_down))
    up_slots = [
        up_pieces[0], up_pieces[1],
        jnp.concatenate(up_pieces[2:4], axis=0), jnp.concatenate(up_pieces[4:], axis=0),
    ]
    part_up = jnp.concatenate(in_order(jnp.stack(up_slots), rank), axis=0)
    d_down = jnp.concatenate(d_down, axis=0)
    attended = unpack_heads(head_exchange(out_packed))

    def to_owners(pieces, parts):
        slots = pieces.astype(BF16).reshape(4, 16, -1)
        slots = jnp.stack([slots[0]] + [swap(slots[s], s) for s in (1, 2, 3)])
        return jnp.stack(in_order(slots, rank)).reshape(4, 16, parts, -1)

    residual_in = tokens[0].astype(F32)
    middle = residual_in + reduce_slots(dot(attended, w_out, 1, 0)) + full_bout
    normed_two, norm_two_back = jax.vjp(layer_norm, middle, gain_two, shift_two)
    normed_two = gather_slots(normed_two.astype(BF16))
    pre_act = dot(normed_two, part_up, 1, 0) + bias_up
    hidden, gelu_back = jax.vjp(gelu_tanh, pre_act)
    hidden = hidden.astype(BF16)
    grad_wdown = dot(hidden, d_down, 0, 0).astype(BF16).reshape(16, 64, 1024)

    (d_pre,) = gelu_back(dot(d_down, w_down, 1, 1))
    d_pre, grad_wdown = lax.optimization_barrier((d_pre.astype(BF16), grad_wdown))
    grad_wdown = head_exchange(grad_wdown)
    d_normed_two = reduce_slots(dot(d_pre, part_up, 1, 1))
    d_norm_two, grad_gain_two, grad_shift_two = norm_two_back(d_normed_two)
    d_output = cotangent[0].astype(F32)
    d_middle = d_output + d_norm_two
    d_branch_own = d_middle.astype(BF16)
    d_branch = gather_slots(d_branch_own)
    d_attended = dot(d_branch, w_out, 1, 1)

    d_packed, grad_wdown = lax.optimization_barrier((pack_heads(d_attended), grad_wdown))
    grad = head_exchange(d_packed)
    early = early_pieces(rank_scalar, normed_two, d_pre, attended, d_branch)
    grad, early = lax.optimization_barrier((grad, early))
    early = head_exchange(early)
    grad_wdown = plane_gather(plane_sum(grad_wdown).astype(BF16))
    dkv_other, dq, d_out, delta = back_other(
        own_sorted, other_sorted, grad, q, k_other, v_other, exact, logs
    )
    dkv_other = partner(dkv_other)
    dq, dkv_own = back_own(own_sorted, d_out, q, k_own, v_own, delta, logs, dq)
    dkv = (dkv_own + dkv_other.astype(F32)).astype(BF16)
    d_packed = jnp.concatenate([dq, dkv], axis=2)
    d_packed, early, hidden = lax.optimization_barrier((d_packed, early, hidden))
    d_packed = head_exchange(d_packed)
    output = middle + reduce_slots(dot(hidden, w_down, 1, 0)) + full_bdown
    early = plane_sum(early)
    up_rows = to_owners(early[:64], 1).reshape(64, 1024)
    early = plane_gather(jnp.concatenate([up_rows, early[64:].astype(BF16)], axis=0))
    d_mixed, late = late_pieces(rank_scalar, d_packed, normed_one)
    late = head_exchange(late)
    d_normed_one = reduce_slots(dot(d_mixed, part_qkv, 1, 1))
    _, norm_one_back = jax.vjp(layer_norm, residual_in, gain_one, shift_one)
    d_norm_one, grad_gain_one, grad_shift_one = norm_one_back(d_normed_one)
    grad_input = d_middle + d_norm_one

    sums = jnp.sum(d_mixed.astype(F32), axis=0)
    grad_bqv = jnp.zeros((2048,), F32)
    grad_bqv = lax.dynamic_update_slice_in_dim(grad_bqv, sums[:256], rank * 256, 0)
    grad_bqv = lax.dynamic_update_slice_in_dim(grad_bqv, sums[512:], 1024 + rank * 256, 0)
    grad_bup = lax.dynamic_update_slice_in_dim(
        jnp.zeros((4, 1024), F32), jnp.sum(d_pre.astype(F32), axis=0)[None], rank, 0
    )
    vectors = jnp.concatenate(
        [
            grad_bqv.reshape(4, 512),
            jnp.sum(d_branch_own.astype(F32), axis=0).reshape(4, 256),
            grad_gain_one.reshape(4, 256),
            grad_shift_one.reshape(4, 256),
            grad_gain_two.reshape(4, 256),
            grad_shift_two.reshape(4, 256),
            grad_bup,
            jnp.sum(d_output, axis=0).reshape(4, 256),
        ],
        axis=1,
    )
    vectors = jnp.stack(in_order(vectors, rank)).reshape(4, 24, 128).astype(BF16)
    vectors = vectors.astype(F32) + partner(vectors).astype(F32)
    vector = vectors[0]
    for slot in (1, 2, 3):
        vector = vector + swap(vectors[slot].astype(BF16), slot).astype(F32)
    late, vector = lax.optimization_barrier((late, vector))
    late = to_owners(plane_sum(late), 3).reshape(4, 16, 3, 2, 128)
    late = late.transpose(2, 0, 3, 1, 4).reshape(384, 128)
    late, grad_wdown = lax.optimization_barrier((late, grad_wdown))
    late = spread(jnp.concatenate([late, vector.astype(BF16)], axis=0))

    out_wdown = grad_wdown.reshape(1024, 1024).astype(F32)
    out_wup = early[:, :64].astype(F32).reshape(16, 4, 16, 1024)
    out_wup = out_wup.transpose(0, 2, 1, 3).reshape(256, 4096)
    out_wout = early[:, 64:].astype(F32).reshape(256, 1024)
    out_wqkv = late[:, :384].reshape(16, 24, 16, 128).astype(F32)
    out_wqkv = out_wqkv.transpose(0, 2, 1, 3).reshape(256, 3072)
    out_vec = jnp.sum(late[:, 384:].astype(F32), axis=0).reshape(3072)
    return (
        output.astype(BF16)[None],
        grad_input.astype(BF16)[None],
        out_wqkv,
        out_vec[0:512],
        out_wout,
        out_vec[512:768],
        out_vec[768:1024],
        out_vec[1024:1280],
        out_vec[1280:1536],
        out_vec[1536:1792],
        out_wup,
        out_vec[1792:2816],
        out_wdown,
        out_vec[2816:3072],
    )


def solution(mesh):
    rows = P("wsh", "ctx", None)
    matrix = P("wsh", None)
    vector = P("wsh")
    return jax.shard_map(
        body,
        mesh=mesh,
        in_specs=(
            rows, P("wsh", "ctx"), matrix, vector, matrix, vector, vector, vector, vector, vector,
            matrix, vector, matrix, vector, rows,
        ),
        out_specs=(
            rows, rows, matrix, vector, matrix, vector, vector, vector, vector, vector,
            matrix, vector, matrix, vector,
        ),
        check_vma=False,
    )
```

```python
import functools

import jax
import jax.numpy as jnp
import ml_dtypes
import numpy as np
from jax import lax
from jax.experimental import pallas as pl
from jax.experimental.pallas import tpu as pltpu
from jax.sharding import PartitionSpec as P

HEADS = 16
HEAD_DIM = 64
EPS = 1e-05
NEGATIVE = -1e30
RUN = 64
Q_TILE = 512
K_TILE = 512
F32 = jnp.float32
BF16 = jnp.bfloat16
VMEM = pl.BlockSpec(memory_space=pltpu.VMEM)
SMEM = pl.BlockSpec(memory_space=pltpu.SMEM)
PARAMS = pltpu.CompilerParams(vmem_limit_bytes=20 * 1024 * 1024)
SMALL = pltpu.CompilerParams(vmem_limit_bytes=8 * 1024 * 1024)


def layer_norm(values, gain_vec, shift_vec):
    average = jnp.mean(values, axis=-1, keepdims=True)
    centred = values - average
    variance = jnp.mean(centred * centred, axis=-1, keepdims=True)
    return centred * lax.rsqrt(variance + EPS) * gain_vec + shift_vec


def gelu_tanh(values):
    return (
        0.5
        * values
        * (1.0 + jnp.tanh(0.7978845608028654 * (values + 0.044715 * values * values * values)))
    )


def dot(left, right, left_dim, right_dim):
    return lax.dot_general(
        left, right, (((left_dim,), (right_dim,)), ((), ())), preferred_element_type=F32
    )


VECTORS = (
    (0, 4, 0), (4, 2, 2048), (6, 2, 3072), (8, 2, 4096), (10, 2, 5120), (12, 2, 6144),
    (14, 8, 7168), (22, 2, 11264),
)
MESSAGE_ROWS = RUN + 16


def start_kernel(rank_ref, *refs):
    tokens, (w0, w1, w2a, w2b, w3a, w3b), smalls = refs[:4], refs[4:10], refs[10:14]
    out_ref, normed_ref, weight_ref, vector_ref = refs[14:]
    rank = rank_ref[0]
    for slot, parts in enumerate(((w0,), (w1,), (w2a, w2b), (w3a, w3b))):
        owner = jnp.bitwise_xor(rank, slot)
        size = 256 // len(parts)
        small = smalls[slot][...].astype(F32)
        for i, part in enumerate(parts):
            rows = pl.ds(pl.multiple_of(owner * 256 + i * size, size), size)
            weight_ref[rows, :] = part[...]
        for row, count, base in VECTORS:
            for i in range(count):
                at = pl.multiple_of(base + (owner * count + i) * 128, 128)
                vector_ref[:, pl.ds(at, 128)] = small[row + i : row + i + 1, :]
    gain, shift = vector_ref[:, 3072:4096], vector_ref[:, 4096:5120]
    at = pl.multiple_of(rank * 256, 256)
    biases = (
        vector_ref[:, pl.ds(at, 256)],
        jnp.zeros((1, 256), F32),
        vector_ref[:, pl.ds(pl.multiple_of(1024 + rank * 256, 256), 256)],
    )
    lane = lax.broadcasted_iota(jnp.int32, (16, 384), 1)
    for slot in range(4):
        rows = pl.ds(slot * 128, 128)
        normed = layer_norm(tokens[slot][...].astype(F32), gain, shift).astype(BF16)
        normed_ref[rows, :] = normed
        mixed = dot(normed, weight_ref[...], 1, 0)
        mixed = [mixed[:, part * 256 : part * 256 + 256] + biases[part] for part in range(3)]
        runs = smalls[slot][...].astype(F32)[24:25, :]
        runs = jnp.where(lane % 2 == 0, runs[:, 0:1], runs[:, 1:2]).astype(BF16)
        for head in range(4):
            cols = slice(head * HEAD_DIM, (head + 1) * HEAD_DIM)
            qe, ke, ve = (part[:RUN, cols] for part in mixed)
            ql, kl, vl = (part[RUN:, cols] for part in mixed)
            message = jnp.concatenate([qe, ql, ke, ve, kl, vl], axis=1).astype(BF16)
            out_ref[slot * 4 + head, :RUN, :] = message
            out_ref[slot * 4 + head, RUN:, :] = runs


def start(rank, tokens, weights, smalls):
    args = (rank, *tokens, *weights, *smalls)
    return pl.pallas_call(
        start_kernel,
        out_shape=(
            jax.ShapeDtypeStruct((16, MESSAGE_ROWS, 384), BF16),
            jax.ShapeDtypeStruct((512, 1024), BF16),
            jax.ShapeDtypeStruct((1024, 768), BF16),
            jax.ShapeDtypeStruct((1, 12288), F32),
        ),
        in_specs=[SMEM] + [VMEM] * (len(args) - 1),
        out_specs=(VMEM,) * 4,
        compiler_params=PARAMS,
    )(*args)


def pack_heads_kernel(flat_ref, out_ref):
    for slot in range(4):
        for head in range(4):
            cols = pl.ds(head * HEAD_DIM, HEAD_DIM)
            out_ref[slot * 4 + head] = jnp.concatenate(
                [
                    flat_ref[pl.ds(slot * 128, RUN), cols],
                    flat_ref[pl.ds(slot * 128 + RUN, RUN), cols],
                ],
                axis=1,
            ).astype(BF16)


def pack_heads(flat):
    return pl.pallas_call(
        pack_heads_kernel,
        out_shape=jax.ShapeDtypeStruct((16, RUN, 128), BF16),
        in_specs=[VMEM],
        out_specs=VMEM,
        compiler_params=SMALL,
    )(flat)


def unpack_heads_kernel(packed_ref, out_ref):
    for slot in range(4):
        for half in range(2):
            rows = pl.ds(slot * 128 + half * RUN, RUN)
            out_ref[rows, :] = jnp.concatenate(
                [
                    packed_ref[slot * 4 + head, :, pl.ds(half * HEAD_DIM, HEAD_DIM)]
                    for head in range(4)
                ],
                axis=1,
            )


def unpack_heads(packed):
    return pl.pallas_call(
        unpack_heads_kernel,
        out_shape=jax.ShapeDtypeStruct((512, 256), BF16),
        in_specs=[VMEM],
        out_specs=VMEM,
        compiler_params=SMALL,
    )(packed)


def by_owner(left, right, rank):
    blocks = []
    for slot in range(4):
        at = pl.multiple_of(jnp.bitwise_xor(rank, slot) * 256, 256)
        blocks.append(dot(left[:, pl.ds(at, 256)], right, 0, 0).astype(BF16))
    return blocks


def late_kernel(rank_ref, packed_ref, normed_ref, mixed_ref, out_ref):
    starts = ((0, 128, 192), (64, 256, 320))
    for slot in range(4):
        for half in range(2):
            parts = [[], [], []]
            for head in range(4):
                for part in range(3):
                    lanes = pl.ds(starts[half][part], HEAD_DIM)
                    parts[part].append(packed_ref[slot * 4 + head, :, lanes])
            rows = pl.ds(slot * 128 + half * RUN, RUN)
            mixed_ref[rows, :] = jnp.concatenate(sum(parts, []), axis=1)
    for slot, block in enumerate(by_owner(normed_ref, mixed_ref[...], rank_ref[0])):
        out_ref[:, slot * 16 : slot * 16 + 16, :] = block.reshape(16, 16, 768)


def late_pieces(rank, packed, normed):
    return pl.pallas_call(
        late_kernel,
        out_shape=(
            jax.ShapeDtypeStruct((512, 768), BF16),
            jax.ShapeDtypeStruct((16, 64, 768), BF16),
        ),
        in_specs=[SMEM, VMEM, VMEM],
        out_specs=(VMEM, VMEM),
        compiler_params=PARAMS,
    )(rank, packed, normed)


def early_kernel(
    rank_ref, normed_ref, d_pre_ref, attended_ref, branch_ref, out_ref
):
    for slot, block in enumerate(by_owner(normed_ref, d_pre_ref[...], rank_ref[0])):
        out_ref[:, slot * 16 : slot * 16 + 16, :] = block.reshape(16, 16, 1024)
    block = dot(attended_ref[...], branch_ref[...], 0, 0).astype(BF16)
    out_ref[:, 64:80, :] = block.reshape(16, 16, 1024)


def early_pieces(*args):
    return pl.pallas_call(
        early_kernel,
        out_shape=jax.ShapeDtypeStruct((16, 80, 1024), BF16),
        in_specs=[SMEM] + [VMEM] * 4,
        out_specs=VMEM,
        compiler_params=PARAMS,
    )(*args)


def spread_early_kernel(packed_ref, up_ref, out_ref):
    for piece in range(16):
        rows = slice(piece * 16, piece * 16 + 16)
        for block in range(4):
            up_ref[rows, block * 1024 : block * 1024 + 1024] = packed_ref[
                piece, block * 16 : block * 16 + 16, :
            ].astype(F32)
        out_ref[rows, :] = packed_ref[piece, 64:80, :].astype(F32)


def spread_early(packed):
    return pl.pallas_call(
        spread_early_kernel,
        out_shape=(
            jax.ShapeDtypeStruct((256, 4096), F32), jax.ShapeDtypeStruct((256, 1024), F32)
        ),
        in_specs=[VMEM],
        out_specs=(VMEM, VMEM),
        compiler_params=PARAMS,
    )(packed)


def spread_late_kernel(packed_ref, qkv_ref, vector_ref):
    for piece in range(16):
        rows = slice(piece * 16, piece * 16 + 16)
        for block in range(24):
            qkv_ref[rows, block * 128 : block * 128 + 128] = packed_ref[
                piece, block * 16 : block * 16 + 16, :
            ].astype(F32)
    vector_ref[...] = jnp.sum(packed_ref[:, 384:, :].astype(F32), axis=0)


def spread_late(packed):
    return pl.pallas_call(
        spread_late_kernel,
        out_shape=(
            jax.ShapeDtypeStruct((256, 3072), F32), jax.ShapeDtypeStruct((32, 128), F32)
        ),
        in_specs=[VMEM],
        out_specs=(VMEM, VMEM),
        compiler_params=PARAMS,
    )(packed)


HALF_ROWS = 2048
RANK, ORDER, SORTED = 0, 40, 80
SLOPES = (8.0 * 2.0 ** (-4.0 * (np.arange(HEADS) + 1.0) / HEADS) / 4096.0).astype(np.float32)


def slope_table():
    rest, parts = SLOPES, []
    for _ in range(3):
        parts.append(rest.astype(ml_dtypes.bfloat16).astype(np.float32))
        rest = rest - parts[-1]
    return np.stack(parts, axis=1).reshape(-1)


def sort_runs(runs_ref, sorted_ref, place_ref):
    for place in range(64):
        place_ref[place] = 32
    for source in range(32):
        place_ref[runs_ref[source]] = source

    def step(place, count):
        source = place_ref[place]
        sorted_ref[RANK + source] = count
        sorted_ref[ORDER + count] = place
        return count + (source < 32).astype(jnp.int32)

    lax.fori_loop(0, 64, step, 0)


def run_rows(index):
    return pl.ds(pl.multiple_of(index * RUN, RUN), RUN)


def tile_rows(index, size):
    return pl.ds(pl.multiple_of(index * size, size), size)


def tile_limits(sorted_ref, tile, own):
    per = Q_TILE // RUN
    lane = lax.broadcasted_iota(jnp.int32, (1, Q_TILE), 1)
    if own:
        lowest = tile * Q_TILE
        return lane + lowest, (lowest + 1) // K_TILE, (lowest + Q_TILE - 1) // K_TILE + 1
    counts = [
        (sorted_ref[ORDER + tile * per + i] - (tile * per + i)) * RUN for i in range(per)
    ]
    limits = jnp.zeros((1, Q_TILE), jnp.int32)
    for i in range(per):
        limits = jnp.where(lane // RUN == i, counts[i] - 1, limits)
    return limits, counts[0] // K_TILE, (counts[per - 1] + K_TILE - 1) // K_TILE


def slope_lanes(head_ref, slope_ref):
    lane = lax.broadcasted_iota(jnp.int32, (RUN, HEAD_DIM), 1)
    lanes = jnp.zeros((RUN, HEAD_DIM), F32)
    for i in range(3):
        slope = slope_ref[head_ref[0] * 3 + i]
        lanes = jnp.where(lane == i, slope * RUN, lanes)
        lanes = jnp.where(lane == 3 + i, slope, lanes)
    return lanes.astype(BF16)


def sort_keys(runs_ref, sorted_ref, packed_ref, first_lane, k_ref, v_ref):
    lane = lax.broadcasted_iota(jnp.int32, (RUN, HEAD_DIM), 1)
    offset = lax.broadcasted_iota(jnp.int32, (RUN, HEAD_DIM), 0)
    for source in range(16):
        for half in range(2):
            index = source * 2 + half
            place = run_rows(sorted_ref[RANK + index])
            lanes = jnp.where(lane < 3, runs_ref[index], offset)
            lanes = jnp.where(lane < 6, lanes, 0).astype(F32).astype(BF16)
            at = first_lane + half * 128
            k_ref[place, :] = jnp.concatenate(
                [packed_ref[source, :RUN, pl.ds(at, HEAD_DIM)], lanes], axis=1
            )
            v_ref[place, :] = packed_ref[source, :RUN, pl.ds(at + HEAD_DIM, HEAD_DIM)]


def transpose_rows(source_ref, target_ref):
    for chunk in range(HALF_ROWS // K_TILE):
        rows = pl.ds(chunk * K_TILE, K_TILE)
        target_ref[:, rows] = source_ref[rows, :HEAD_DIM].T


def loop_chunks(step, limits, carry):
    _, full, every = limits
    if isinstance(every, int):
        for chunk in range(every):
            carry = step(chunk >= full, chunk, carry)
        return carry
    carry = lax.fori_loop(0, full, functools.partial(step, False), carry)
    return lax.fori_loop(full, every, functools.partial(step, True), carry)


def masked_scores(masked, chunk, key, query, limits):
    scores = dot(key, query, 1, 1)
    if masked:
        ramp = lax.broadcasted_iota(jnp.int32, (K_TILE, Q_TILE), 0)
        scores = jnp.where(ramp <= limits[0] - chunk * K_TILE, scores, NEGATIVE)
    return scores


def fold_tile(query, limits, carry, k_ref, vt_ref):
    def step(masked, chunk, carry):
        highest, total, accum = carry
        k_rows = tile_rows(chunk, K_TILE)
        scores = masked_scores(masked, chunk, k_ref[k_rows, :], query, limits)
        new_high = jnp.maximum(highest, jnp.max(scores, axis=0, keepdims=True))
        weights = jnp.exp(scores - new_high)
        factor = jnp.exp(highest - new_high)
        total = total * factor + jnp.sum(weights, axis=0, keepdims=True)
        accum = accum * factor + dot(vt_ref[:, k_rows], weights.astype(BF16), 1, 0)
        return new_high, total, accum

    return loop_chunks(step, limits, carry)


def attend_own_kernel(
    head_ref, slope_ref, runs_ref, own_ref,
    sorted_ref, q_ref, k_ref, v_ref, high_ref, total_ref, accum_ref,
    place_ref, vt_ref,
):
    sort_runs(runs_ref, sorted_ref, place_ref)
    lanes = slope_lanes(head_ref, slope_ref)
    for source in range(16):
        for half in range(2):
            query = own_ref[source, :RUN, pl.ds(half * HEAD_DIM, HEAD_DIM)].astype(F32)
            q_ref[run_rows(sorted_ref[RANK + source * 2 + half]), :] = jnp.concatenate(
                [(query * HEAD_DIM ** (-0.5)).astype(BF16), lanes], axis=1
            )
    sort_keys(runs_ref, sorted_ref, own_ref, 128, k_ref, v_ref)
    transpose_rows(v_ref, vt_ref)

    def tile_step(tile, unused):
        q_rows = tile_rows(tile, Q_TILE)
        carry = (
            jnp.full((1, Q_TILE), NEGATIVE, F32),
            jnp.zeros((1, Q_TILE), F32),
            jnp.zeros((HEAD_DIM, Q_TILE), F32),
        )
        limits = tile_limits(sorted_ref, tile, True)
        carry = fold_tile(q_ref[q_rows, :], limits, carry, k_ref, vt_ref)
        high_ref[:, q_rows], total_ref[:, q_rows], accum_ref[:, q_rows] = carry
        return unused

    for tile in range(HALF_ROWS // Q_TILE):
        tile_step(tile, 0)


def attend_other_kernel(
    own_sorted_ref, runs_ref, other_ref, q_ref, high_ref, total_ref, accum_ref,
    out_ref, sorted_ref, k_ref, v_ref, exact_ref, log_ref,
    place_ref, vt_ref, rows_ref,
):
    sort_runs(runs_ref, sorted_ref, place_ref)
    sort_keys(runs_ref, sorted_ref, other_ref, 0, k_ref, v_ref)
    transpose_rows(v_ref, vt_ref)

    def tile_step(tile, unused):
        q_rows = tile_rows(tile, Q_TILE)
        carry = (high_ref[:, q_rows], total_ref[:, q_rows], accum_ref[:, q_rows])
        limits = tile_limits(own_sorted_ref, tile, False)
        highest, total, accum = fold_tile(q_ref[q_rows, :], limits, carry, k_ref, vt_ref)
        exact = accum / total
        exact_ref[:, q_rows] = exact
        log_ref[:, q_rows] = highest + jnp.log(total)
        rows_ref[q_rows, :] = exact.T
        return unused

    lax.fori_loop(0, HALF_ROWS // Q_TILE, tile_step, 0)
    for source in range(16):
        out_ref[source] = jnp.concatenate(
            [rows_ref[run_rows(own_sorted_ref[RANK + source * 2 + half]), :] for half in range(2)],
            axis=1,
        ).astype(BF16)


def unfold_tile(query, d_out, logs, delta, limits, dq, k_ref, v_ref, kt_ref, dk_ref, dv_ref):
    def step(masked, chunk, dq):
        k_rows = tile_rows(chunk, K_TILE)
        scores = masked_scores(masked, chunk, k_ref[k_rows, :], query, limits)
        weights = jnp.exp(scores - logs)
        d_weights = dot(v_ref[k_rows, :], d_out, 1, 1)
        d_scores = (weights * (d_weights - delta)).astype(BF16)
        dv_ref[k_rows, :] += dot(weights.astype(BF16), d_out, 1, 0)
        dk_ref[k_rows, :] += dot(d_scores, query, 1, 0)
        return dq + dot(kt_ref[:, k_rows], d_scores, 1, 0)

    return loop_chunks(step, limits, dq)


def write_keys(sorted_ref, dk_ref, dv_ref, target):
    for source in range(16):
        parts = []
        for half in range(2):
            place = run_rows(sorted_ref[RANK + source * 2 + half])
            parts += [dk_ref[place, :HEAD_DIM], dv_ref[place, :]]
        target[source] = jnp.concatenate(parts, axis=1).astype(target.dtype)


def back_other_kernel(
    own_sorted_ref, sorted_ref, grad_ref, q_ref, k_ref, v_ref, exact_ref, log_ref,
    other_out, dq_ref, do_ref, delta_ref,
    kt_ref, dk_ref, dv_ref,
):
    for source in range(16):
        for half in range(2):
            do_ref[run_rows(own_sorted_ref[RANK + source * 2 + half]), :] = grad_ref[
                source, :, pl.ds(half * HEAD_DIM, HEAD_DIM)
            ]
    transpose_rows(k_ref, kt_ref)
    dk_ref[...] = jnp.zeros_like(dk_ref)
    dv_ref[...] = jnp.zeros_like(dv_ref)

    def tile_step(tile, unused):
        q_rows = tile_rows(tile, Q_TILE)
        d_out = do_ref[q_rows, :]
        delta = jnp.sum(d_out.astype(F32).T * exact_ref[:, q_rows], axis=0, keepdims=True)
        delta_ref[:, q_rows] = delta
        dq_ref[:, q_rows] = unfold_tile(
            q_ref[q_rows, :], d_out, log_ref[:, q_rows], delta,
            tile_limits(own_sorted_ref, tile, False), jnp.zeros((HEAD_DIM, Q_TILE), F32),
            k_ref, v_ref, kt_ref, dk_ref, dv_ref,
        )
        return unused

    lax.fori_loop(0, HALF_ROWS // Q_TILE, tile_step, 0)
    write_keys(sorted_ref, dk_ref, dv_ref, other_out)


def back_own_kernel(
    sorted_ref, do_ref, q_ref, k_ref, v_ref, delta_ref, log_ref, dq_ref,
    dq_out, own_out,
    kt_ref, rows_ref, dk_ref, dv_ref,
):
    transpose_rows(k_ref, kt_ref)
    dk_ref[...] = jnp.zeros_like(dk_ref)
    dv_ref[...] = jnp.zeros_like(dv_ref)

    def tile_step(tile, unused):
        q_rows = tile_rows(tile, Q_TILE)
        dq = unfold_tile(
            q_ref[q_rows, :], do_ref[q_rows, :], log_ref[:, q_rows], delta_ref[:, q_rows],
            tile_limits(sorted_ref, tile, True), dq_ref[:, q_rows],
            k_ref, v_ref, kt_ref, dk_ref, dv_ref,
        )
        rows_ref[q_rows, :] = (dq * HEAD_DIM ** (-0.5)).T
        return unused

    for tile in range(HALF_ROWS // Q_TILE):
        tile_step(tile, 0)
    for source in range(16):
        dq_out[source] = jnp.concatenate(
            [rows_ref[run_rows(sorted_ref[RANK + source * 2 + half]), :] for half in range(2)],
            axis=1,
        ).astype(BF16)
    write_keys(sorted_ref, dk_ref, dv_ref, own_out)


def shape(*dims, dtype=F32):
    return jax.ShapeDtypeStruct(dims, dtype)


def call_attention(kernel, args, outs, scratch, smem):
    return pl.pallas_call(
        kernel,
        out_shape=outs,
        in_specs=[SMEM] * smem + [VMEM] * (len(args) - smem),
        out_specs=tuple(SMEM if out.dtype == jnp.int32 else VMEM for out in outs),
        scratch_shapes=scratch,
        compiler_params=PARAMS,
        cost_estimate=pl.CostEstimate(
            flops=12_000_000_000, bytes_accessed=4_000_000, transcendentals=4_000_000
        ),
    )(*args)


Q_SHAPE = shape(HALF_ROWS, 128, dtype=BF16)
V_SHAPE = shape(HALF_ROWS, HEAD_DIM, dtype=BF16)
ROW_SHAPE = shape(1, HALF_ROWS)
COLUMN_SHAPE = shape(HEAD_DIM, HALF_ROWS)
FLIPPED = pltpu.VMEM((HEAD_DIM, HALF_ROWS), BF16)
NARROW = pltpu.VMEM((HALF_ROWS, HEAD_DIM), F32)
WIDE = pltpu.VMEM((HALF_ROWS, 128), F32)


SORTED_SHAPE = shape(SORTED, dtype=jnp.int32)
PLACES = pltpu.SMEM((64,), jnp.int32)


def attend_own(*args):
    outs = (SORTED_SHAPE, Q_SHAPE, Q_SHAPE, V_SHAPE, ROW_SHAPE, ROW_SHAPE, COLUMN_SHAPE)
    return call_attention(attend_own_kernel, args, outs, [PLACES, FLIPPED], 3)


def attend_other(*args):
    outs = (shape(16, RUN, 128, dtype=BF16), SORTED_SHAPE, Q_SHAPE, V_SHAPE, COLUMN_SHAPE, ROW_SHAPE)
    return call_attention(attend_other_kernel, args, outs, [PLACES, FLIPPED, NARROW], 2)


def back_other(*args):
    outs = (shape(16, RUN, 256, dtype=BF16), COLUMN_SHAPE, V_SHAPE, ROW_SHAPE)
    return call_attention(back_other_kernel, args, outs, [FLIPPED, WIDE, NARROW], 2)


def back_own(*args):
    outs = (shape(16, RUN, 128, dtype=BF16), shape(16, RUN, 256))
    return call_attention(back_own_kernel, args, outs, [FLIPPED, NARROW, WIDE, NARROW], 1)


PLANES = [[2 * i + z for i in range(16)] for z in range(2)]


def swap(value, slot):
    return lax.ppermute(value, "wsh", [(i, i ^ slot) for i in range(4)])


def gather_list(value):
    across = swap(value, 2)
    return [value, swap(value, 1), across, swap(across, 1)]


def gather_slots(value):
    return jnp.concatenate(gather_list(value), axis=0)


def swap_weight(weight, rank, starts, size):
    def columns(slot, row, rows):
        parts = [
            lax.dynamic_slice(
                weight, (row, start + jnp.bitwise_xor(rank, slot) * size), (rows, size)
            )
            for start in starts
        ]
        return jnp.concatenate(parts, axis=1) if len(parts) > 1 else parts[0]

    pieces = [columns(0, 0, 256), columns(1, 0, 256)]
    pieces += [columns(slot, row, 128) for slot in (2, 3) for row in (0, 128)]
    return pieces


def swap_pieces(pieces):
    def wrapped(slot):
        return [(c * 4 + r, (c ^ 1) * 4 + (r ^ slot)) for c in range(32) for r in range(4)]

    return [
        pieces[0], swap(pieces[1], 1),
        swap(pieces[2], 2), lax.ppermute(pieces[3], ("ctx", "wsh"), wrapped(2)),
        swap(pieces[4], 3), lax.ppermute(pieces[5], ("ctx", "wsh"), wrapped(3)),
    ]


def reduce_slots(partial):
    rows = partial.reshape(4, 128, -1)
    across = rows[2] + swap(rows[3].astype(BF16), 1).astype(F32)
    across = swap(across.astype(BF16), 2).astype(F32)
    return rows[0] + swap(rows[1].astype(BF16), 1).astype(F32) + across


def in_order(slots, rank):
    return [
        lax.dynamic_index_in_dim(slots, jnp.bitwise_xor(rank, i), 0, keepdims=False)
        for i in range(4)
    ]


def head_exchange(value):
    return lax.all_to_all(value, "ctx", 0, 0, axis_index_groups=PLANES, tiled=True)


def partner(value):
    return lax.ppermute(value, "ctx", [(i, i ^ 1) for i in range(32)])


def plane_sum(received):
    total = jnp.sum(received.astype(F32), axis=0).astype(BF16)
    return total.astype(F32) + partner(total).astype(F32)


def plane_gather(shard):
    return lax.all_gather(shard, "ctx", axis=0, axis_index_groups=PLANES)


def spread(shard):
    rows = jnp.broadcast_to(shard, (16,) + shard.shape)
    return head_exchange(rows).reshape(rows.shape)


def body(
    tokens,
    places,
    w_qkv,
    b_qv,
    w_out,
    b_out,
    norm1_gain,
    norm1_shift,
    norm2_gain,
    norm2_shift,
    w_up,
    b_up,
    w_down,
    b_down,
    cotangent,
):
    rank = lax.axis_index("wsh")
    column = lax.axis_index("ctx")
    head = rank * 4 + (column // 2) % 4
    rank_scalar = rank.astype(jnp.int32).reshape(1)

    pieces = swap_weight(w_qkv, rank, (0, 1024, 2048), 256)
    vectors = (b_qv, b_out, norm1_gain, norm1_shift, norm2_gain, norm2_shift, b_up, b_down)
    pieces, vectors, places = lax.optimization_barrier((pieces, vectors, places))
    pieces = swap_pieces(pieces)
    runs = (places[0].reshape(2, RUN)[:, 0] // RUN).astype(BF16)
    small = [item.reshape(-1, 128) for item in vectors]
    small = jnp.concatenate(small + [jnp.pad(runs.reshape(1, 2), ((0, 0), (0, 126)))], axis=0)
    smalls = [small] + [swap(small, slot) for slot in (1, 2, 3)]
    smalls, w_up, cotangent = lax.optimization_barrier((smalls, w_up, cotangent))
    packed, normed_one, part_qkv, vector = start(
        rank_scalar, gather_list(tokens[0]), pieces, smalls
    )
    full_bout = vector[0, 2048:3072]
    gain_one = vector[0, 3072:4096]
    shift_one = vector[0, 4096:5120]
    gain_two = vector[0, 5120:6144]
    shift_two = vector[0, 6144:7168]
    bias_up = lax.dynamic_slice_in_dim(vector, 7168 + rank * 1024, 1024, 1)
    full_bdown = vector[0, 11264:]

    own = head_exchange(packed)

    up_pieces = swap_pieces(swap_weight(w_up, rank, (0,), 1024))
    d_down = gather_list(cotangent[0])

    def run_indices(message):
        return message[:, RUN, :2].astype(jnp.int32).reshape(32)

    other = partner(own[:, :, 128:])
    own_sorted, q, k_own, v_own, *state = attend_own(
        head.astype(jnp.int32).reshape(1), slope_table(), run_indices(own), own
    )
    out_packed, other_sorted, k_other, v_other, exact, logs = attend_other(
        own_sorted, run_indices(other), other, q, *state
    )
    out_packed, up_pieces, d_down = lax.optimization_barrier((out_packed, up_pieces, d_down))
    up_slots = [
        up_pieces[0], up_pieces[1],
        jnp.concatenate(up_pieces[2:4], axis=0), jnp.concatenate(up_pieces[4:], axis=0),
    ]
    part_up = jnp.concatenate(in_order(jnp.stack(up_slots), rank), axis=0)
    d_down = jnp.concatenate(d_down, axis=0)
    attended = unpack_heads(head_exchange(out_packed))

    def to_owners(pieces, parts):
        slots = pieces.astype(BF16).reshape(4, 16, -1)
        slots = jnp.stack([slots[0]] + [swap(slots[s], s) for s in (1, 2, 3)])
        columns = jnp.stack(in_order(slots, rank))
        return columns if parts == 1 else columns.reshape(4, 16, parts, -1)

    residual_in = tokens[0].astype(F32)
    middle = residual_in + reduce_slots(dot(attended, w_out, 1, 0)) + full_bout
    normed_two, norm_two_back = jax.vjp(layer_norm, middle, gain_two, shift_two)
    normed_two = gather_slots(normed_two.astype(BF16))
    pre_act = dot(normed_two, part_up, 1, 0) + bias_up
    hidden, gelu_back = jax.vjp(gelu_tanh, pre_act)
    hidden = hidden.astype(BF16)
    grad_wdown = dot(hidden, d_down, 0, 0).astype(BF16).reshape(16, 64, 1024)

    (d_pre,) = gelu_back(dot(d_down, w_down, 1, 1))
    d_pre, grad_wdown = lax.optimization_barrier((d_pre.astype(BF16), grad_wdown))
    grad_wdown = head_exchange(grad_wdown)
    d_normed_two = reduce_slots(dot(d_pre, part_up, 1, 1))
    d_norm_two, grad_gain_two, grad_shift_two = norm_two_back(d_normed_two)
    d_output = cotangent[0].astype(F32)
    d_middle = d_output + d_norm_two
    d_branch_own = d_middle.astype(BF16)
    d_branch = gather_slots(d_branch_own)
    d_attended = dot(d_branch, w_out, 1, 1)

    d_packed, grad_wdown = lax.optimization_barrier((pack_heads(d_attended), grad_wdown))
    grad = head_exchange(d_packed)
    early = early_pieces(rank_scalar, normed_two, d_pre, attended, d_branch)
    grad, early = lax.optimization_barrier((grad, early))
    early = head_exchange(early)
    grad_wdown = plane_gather(plane_sum(grad_wdown).astype(BF16))
    dkv_other, dq, d_out, delta = back_other(
        own_sorted, other_sorted, grad, q, k_other, v_other, exact, logs
    )
    dkv_other = partner(dkv_other)
    dq, dkv_own = back_own(own_sorted, d_out, q, k_own, v_own, delta, logs, dq)
    dkv = (dkv_own + dkv_other.astype(F32)).astype(BF16)
    d_packed = jnp.concatenate([dq, dkv], axis=2)
    d_packed, early, hidden = lax.optimization_barrier((d_packed, early, hidden))
    d_packed = head_exchange(d_packed)
    output = middle + reduce_slots(dot(hidden, w_down, 1, 0)) + full_bdown
    early = plane_sum(early)
    up_rows = to_owners(early[:64], 1).reshape(64, 1024)
    early = plane_gather(jnp.concatenate([up_rows, early[64:].astype(BF16)], axis=0))
    d_mixed, late = late_pieces(rank_scalar, d_packed, normed_one)
    late = head_exchange(late)
    d_normed_one = reduce_slots(dot(d_mixed, part_qkv, 1, 1))
    _, norm_one_back = jax.vjp(layer_norm, residual_in, gain_one, shift_one)
    d_norm_one, grad_gain_one, grad_shift_one = norm_one_back(d_normed_one)
    grad_input = d_middle + d_norm_one

    sums = jnp.sum(d_mixed.astype(F32), axis=0)
    grad_bqv = jnp.zeros((2048,), F32)
    grad_bqv = lax.dynamic_update_slice_in_dim(grad_bqv, sums[:256], rank * 256, 0)
    grad_bqv = lax.dynamic_update_slice_in_dim(grad_bqv, sums[512:], 1024 + rank * 256, 0)
    grad_bup = lax.dynamic_update_slice_in_dim(
        jnp.zeros((4, 1024), F32), jnp.sum(d_pre.astype(F32), axis=0)[None], rank, 0
    )
    vectors = jnp.concatenate(
        [
            grad_bqv.reshape(4, 512),
            jnp.sum(d_branch_own.astype(F32), axis=0).reshape(4, 256),
            grad_gain_one.reshape(4, 256),
            grad_shift_one.reshape(4, 256),
            grad_gain_two.reshape(4, 256),
            grad_shift_two.reshape(4, 256),
            grad_bup,
            jnp.sum(d_output, axis=0).reshape(4, 256),
        ],
        axis=1,
    )
    vectors = jnp.stack(in_order(vectors, rank)).reshape(4, 24, 128).astype(BF16)
    vectors = vectors.astype(F32) + partner(vectors).astype(F32)
    vector = vectors[0]
    for slot in (1, 2, 3):
        vector = vector + swap(vectors[slot].astype(BF16), slot).astype(F32)
    late, vector = lax.optimization_barrier((late, vector))
    late = to_owners(plane_sum(late), 3).reshape(4, 16, 3, 2, 128)
    late = late.transpose(2, 0, 3, 1, 4).reshape(384, 128)
    late, grad_wdown = lax.optimization_barrier((late, grad_wdown))
    vector = jnp.pad(vector.astype(BF16), ((0, 8), (0, 0)))
    late = spread(jnp.concatenate([late, vector], axis=0))

    out_wdown = grad_wdown.reshape(1024, 1024).astype(F32)
    out_wup, out_wout = spread_early(early)
    out_wqkv, out_vec = spread_late(late)
    out_vec = out_vec[:24].reshape(3072)
    return (
        output.astype(BF16)[None],
        grad_input.astype(BF16)[None],
        out_wqkv,
        out_vec[0:512],
        out_wout,
        out_vec[512:768],
        out_vec[768:1024],
        out_vec[1024:1280],
        out_vec[1280:1536],
        out_vec[1536:1792],
        out_wup,
        out_vec[1792:2816],
        out_wdown,
        out_vec[2816:3072],
    )


def solution(mesh):
    rows = P("wsh", "ctx", None)
    matrix = P("wsh", None)
    vector = P("wsh")
    return jax.shard_map(
        body,
        mesh=mesh,
        in_specs=(
            rows, P("wsh", "ctx"), matrix, vector, matrix, vector, vector, vector, vector, vector,
            matrix, vector, matrix, vector, rows,
        ),
        out_specs=(
            rows, rows, matrix, vector, matrix, vector, vector, vector, vector, vector,
            matrix, vector, matrix, vector,
        ),
        check_vma=False,
    )
```

```python
import functools

import jax
import jax.numpy as jnp
import ml_dtypes
import numpy as np
from jax import lax
from jax.experimental import pallas as pl
from jax.experimental.pallas import tpu as pltpu
from jax.sharding import PartitionSpec as P

HEADS = 16
HEAD_DIM = 64
EPS = 1e-05
NEGATIVE = -1e30
RUN = 64
Q_TILE = 512
K_TILE = 512
F32 = jnp.float32
BF16 = jnp.bfloat16
VMEM = pl.BlockSpec(memory_space=pltpu.VMEM)
SMEM = pl.BlockSpec(memory_space=pltpu.SMEM)
PARAMS = pltpu.CompilerParams(vmem_limit_bytes=20 * 1024 * 1024)
SMALL = pltpu.CompilerParams(vmem_limit_bytes=8 * 1024 * 1024)


def layer_norm(values, gain_vec, shift_vec):
    average = jnp.mean(values, axis=-1, keepdims=True)
    centred = values - average
    variance = jnp.mean(centred * centred, axis=-1, keepdims=True)
    return centred * lax.rsqrt(variance + EPS) * gain_vec + shift_vec


def gelu_tanh(values):
    return (
        0.5
        * values
        * (1.0 + jnp.tanh(0.7978845608028654 * (values + 0.044715 * values * values * values)))
    )


def dot(left, right, left_dim, right_dim):
    return lax.dot_general(
        left, right, (((left_dim,), (right_dim,)), ((), ())), preferred_element_type=F32
    )


VECTORS = (
    (0, 4, 0), (4, 2, 2048), (6, 2, 3072), (8, 2, 4096), (10, 2, 5120), (12, 2, 6144),
    (14, 8, 7168), (22, 2, 11264),
)
MESSAGE_ROWS = RUN + 16


def start_kernel(rank_ref, *refs):
    tokens, (w0, w1, w2a, w2b, w3a, w3b), smalls = refs[:4], refs[4:10], refs[10:14]
    out_ref, normed_ref, weight_ref, vector_ref = refs[14:]
    rank = rank_ref[0]
    for slot, parts in enumerate(((w0,), (w1,), (w2a, w2b), (w3a, w3b))):
        owner = jnp.bitwise_xor(rank, slot)
        size = 256 // len(parts)
        small = smalls[slot][...].astype(F32)
        for i, part in enumerate(parts):
            rows = pl.ds(pl.multiple_of(owner * 256 + i * size, size), size)
            weight_ref[rows, :] = part[...]
        for row, count, base in VECTORS:
            for i in range(count):
                at = pl.multiple_of(base + (owner * count + i) * 128, 128)
                vector_ref[:, pl.ds(at, 128)] = small[row + i : row + i + 1, :]
    gain, shift = vector_ref[:, 3072:4096], vector_ref[:, 4096:5120]
    at = pl.multiple_of(rank * 256, 256)
    biases = (
        vector_ref[:, pl.ds(at, 256)],
        jnp.zeros((1, 256), F32),
        vector_ref[:, pl.ds(pl.multiple_of(1024 + rank * 256, 256), 256)],
    )
    lane = lax.broadcasted_iota(jnp.int32, (16, 384), 1)
    for slot in range(4):
        rows = pl.ds(slot * 128, 128)
        normed = layer_norm(tokens[slot][...].astype(F32), gain, shift).astype(BF16)
        normed_ref[rows, :] = normed
        mixed = dot(normed, weight_ref[...], 1, 0)
        mixed = [mixed[:, part * 256 : part * 256 + 256] + biases[part] for part in range(3)]
        runs = smalls[slot][...].astype(F32)[24:25, :]
        runs = jnp.where(lane % 2 == 0, runs[:, 0:1], runs[:, 1:2]).astype(BF16)
        for head in range(4):
            cols = slice(head * HEAD_DIM, (head + 1) * HEAD_DIM)
            qe, ke, ve = (part[:RUN, cols] for part in mixed)
            ql, kl, vl = (part[RUN:, cols] for part in mixed)
            message = jnp.concatenate([qe, ql, ke, ve, kl, vl], axis=1).astype(BF16)
            out_ref[slot * 4 + head, :RUN, :] = message
            out_ref[slot * 4 + head, RUN:, :] = runs


def start(rank, tokens, weights, smalls):
    args = (rank, *tokens, *weights, *smalls)
    return pl.pallas_call(
        start_kernel,
        out_shape=(
            jax.ShapeDtypeStruct((16, MESSAGE_ROWS, 384), BF16),
            jax.ShapeDtypeStruct((512, 1024), BF16),
            jax.ShapeDtypeStruct((1024, 768), BF16),
            jax.ShapeDtypeStruct((1, 12288), F32),
        ),
        in_specs=[SMEM] + [VMEM] * (len(args) - 1),
        out_specs=(VMEM,) * 4,
        compiler_params=PARAMS,
    )(*args)


def pack_heads_kernel(flat_ref, out_ref):
    for slot in range(4):
        for head in range(4):
            cols = pl.ds(head * HEAD_DIM, HEAD_DIM)
            out_ref[slot * 4 + head] = jnp.concatenate(
                [
                    flat_ref[pl.ds(slot * 128, RUN), cols],
                    flat_ref[pl.ds(slot * 128 + RUN, RUN), cols],
                ],
                axis=1,
            ).astype(BF16)


def pack_heads(flat):
    return pl.pallas_call(
        pack_heads_kernel,
        out_shape=jax.ShapeDtypeStruct((16, RUN, 128), BF16),
        in_specs=[VMEM],
        out_specs=VMEM,
        compiler_params=SMALL,
    )(flat)


def unpack_heads_kernel(packed_ref, out_ref):
    for slot in range(4):
        for half in range(2):
            rows = pl.ds(slot * 128 + half * RUN, RUN)
            out_ref[rows, :] = jnp.concatenate(
                [
                    packed_ref[slot * 4 + head, :, pl.ds(half * HEAD_DIM, HEAD_DIM)]
                    for head in range(4)
                ],
                axis=1,
            )


def unpack_heads(packed):
    return pl.pallas_call(
        unpack_heads_kernel,
        out_shape=jax.ShapeDtypeStruct((512, 256), BF16),
        in_specs=[VMEM],
        out_specs=VMEM,
        compiler_params=SMALL,
    )(packed)


def by_owner(left, right, rank):
    blocks = []
    for slot in range(4):
        at = pl.multiple_of(jnp.bitwise_xor(rank, slot) * 256, 256)
        blocks.append(dot(left[:, pl.ds(at, 256)], right, 0, 0).astype(BF16))
    return blocks


def late_kernel(rank_ref, packed_ref, normed_ref, mixed_ref, out_ref):
    starts = ((0, 128, 192), (64, 256, 320))
    for slot in range(4):
        for half in range(2):
            parts = [[], [], []]
            for head in range(4):
                for part in range(3):
                    lanes = pl.ds(starts[half][part], HEAD_DIM)
                    parts[part].append(packed_ref[slot * 4 + head, :, lanes])
            rows = pl.ds(slot * 128 + half * RUN, RUN)
            mixed_ref[rows, :] = jnp.concatenate(sum(parts, []), axis=1)
    for slot, block in enumerate(by_owner(normed_ref, mixed_ref[...], rank_ref[0])):
        out_ref[:, slot * 16 : slot * 16 + 16, :] = block.reshape(16, 16, 768)


def late_pieces(rank, packed, normed):
    return pl.pallas_call(
        late_kernel,
        out_shape=(
            jax.ShapeDtypeStruct((512, 768), BF16),
            jax.ShapeDtypeStruct((16, 64, 768), BF16),
        ),
        in_specs=[SMEM, VMEM, VMEM],
        out_specs=(VMEM, VMEM),
        compiler_params=PARAMS,
    )(rank, packed, normed)


def early_kernel(
    rank_ref, normed_ref, d_pre_ref, attended_ref, branch_ref, out_ref
):
    for slot, block in enumerate(by_owner(normed_ref, d_pre_ref[...], rank_ref[0])):
        out_ref[:, slot * 16 : slot * 16 + 16, :] = block.reshape(16, 16, 1024)
    block = dot(attended_ref[...], branch_ref[...], 0, 0).astype(BF16)
    out_ref[:, 64:80, :] = block.reshape(16, 16, 1024)


def early_pieces(*args):
    return pl.pallas_call(
        early_kernel,
        out_shape=jax.ShapeDtypeStruct((16, 80, 1024), BF16),
        in_specs=[SMEM] + [VMEM] * 4,
        out_specs=VMEM,
        compiler_params=PARAMS,
    )(*args)


def spread_early_kernel(packed_ref, up_ref, out_ref):
    for piece in range(16):
        rows = slice(piece * 16, piece * 16 + 16)
        for block in range(4):
            up_ref[rows, block * 1024 : block * 1024 + 1024] = packed_ref[
                piece, block * 16 : block * 16 + 16, :
            ].astype(F32)
        out_ref[rows, :] = packed_ref[piece, 64:80, :].astype(F32)


def spread_early(packed):
    return pl.pallas_call(
        spread_early_kernel,
        out_shape=(
            jax.ShapeDtypeStruct((256, 4096), F32), jax.ShapeDtypeStruct((256, 1024), F32)
        ),
        in_specs=[VMEM],
        out_specs=(VMEM, VMEM),
        compiler_params=PARAMS,
    )(packed)


def spread_late_kernel(packed_ref, qkv_ref, vector_ref):
    for piece in range(16):
        rows = slice(piece * 16, piece * 16 + 16)
        for block in range(24):
            qkv_ref[rows, block * 128 : block * 128 + 128] = packed_ref[
                piece, block * 16 : block * 16 + 16, :
            ].astype(F32)
    vector_ref[...] = jnp.sum(packed_ref[:, 384:, :].astype(F32), axis=0)


def spread_late(packed):
    return pl.pallas_call(
        spread_late_kernel,
        out_shape=(
            jax.ShapeDtypeStruct((256, 3072), F32), jax.ShapeDtypeStruct((32, 128), F32)
        ),
        in_specs=[VMEM],
        out_specs=(VMEM, VMEM),
        compiler_params=PARAMS,
    )(packed)


HALF_ROWS = 2048
RANK, ORDER, SORTED = 0, 40, 80
SLOPES = (8.0 * 2.0 ** (-4.0 * (np.arange(HEADS) + 1.0) / HEADS) / 4096.0).astype(np.float32)


def slope_table():
    rest, parts = SLOPES, []
    for _ in range(3):
        parts.append(rest.astype(ml_dtypes.bfloat16).astype(np.float32))
        rest = rest - parts[-1]
    return np.stack(parts, axis=1).reshape(-1)


def sort_runs(runs_ref, sorted_ref, place_ref):
    for place in range(64):
        place_ref[place] = 32
    for source in range(32):
        place_ref[runs_ref[source]] = source

    def step(place, count):
        source = place_ref[place]
        sorted_ref[RANK + source] = count
        sorted_ref[ORDER + count] = place
        return count + (source < 32).astype(jnp.int32)

    lax.fori_loop(0, 64, step, 0)


def run_rows(index):
    return pl.ds(pl.multiple_of(index * RUN, RUN), RUN)


def tile_rows(index, size):
    return pl.ds(pl.multiple_of(index * size, size), size)


def tile_limits(sorted_ref, tile, own):
    per = Q_TILE // RUN
    lane = lax.broadcasted_iota(jnp.int32, (1, Q_TILE), 1)
    if own:
        lowest = tile * Q_TILE
        return lane + lowest, (lowest + 1) // K_TILE, (lowest + Q_TILE - 1) // K_TILE + 1
    counts = [
        (sorted_ref[ORDER + tile * per + i] - (tile * per + i)) * RUN for i in range(per)
    ]
    limits = jnp.zeros((1, Q_TILE), jnp.int32)
    for i in range(per):
        limits = jnp.where(lane // RUN == i, counts[i] - 1, limits)
    return limits, counts[0] // K_TILE, (counts[per - 1] + K_TILE - 1) // K_TILE


def slope_lanes(head_ref, slope_ref):
    lane = lax.broadcasted_iota(jnp.int32, (RUN, HEAD_DIM), 1)
    lanes = jnp.zeros((RUN, HEAD_DIM), F32)
    for i in range(3):
        slope = slope_ref[head_ref[0] * 3 + i]
        lanes = jnp.where(lane == i, slope * RUN, lanes)
        lanes = jnp.where(lane == 3 + i, slope, lanes)
    return lanes.astype(BF16)


def sort_keys(runs_ref, sorted_ref, packed_ref, first_lane, k_ref, v_ref):
    lane = lax.broadcasted_iota(jnp.int32, (RUN, HEAD_DIM), 1)
    offset = lax.broadcasted_iota(jnp.int32, (RUN, HEAD_DIM), 0)
    for source in range(16):
        for half in range(2):
            index = source * 2 + half
            place = run_rows(sorted_ref[RANK + index])
            lanes = jnp.where(lane < 3, runs_ref[index], offset)
            lanes = jnp.where(lane < 6, lanes, 0).astype(F32).astype(BF16)
            at = first_lane + half * 128
            k_ref[place, :] = jnp.concatenate(
                [packed_ref[source, :RUN, pl.ds(at, HEAD_DIM)], lanes], axis=1
            )
            v_ref[place, :] = packed_ref[source, :RUN, pl.ds(at + HEAD_DIM, HEAD_DIM)]


def transpose_rows(source_ref, target_ref):
    for chunk in range(HALF_ROWS // K_TILE):
        rows = pl.ds(chunk * K_TILE, K_TILE)
        target_ref[:, rows] = source_ref[rows, :HEAD_DIM].T


def loop_chunks(step, limits, carry):
    _, full, every = limits
    if isinstance(every, int):
        for chunk in range(every):
            carry = step(chunk >= full, chunk, carry)
        return carry
    carry = lax.fori_loop(0, full, functools.partial(step, False), carry)
    return lax.fori_loop(full, every, functools.partial(step, True), carry)


def masked_scores(masked, chunk, key, query, limits):
    scores = dot(key, query, 1, 1)
    if masked:
        ramp = lax.broadcasted_iota(jnp.int32, (K_TILE, Q_TILE), 0)
        scores = jnp.where(ramp <= limits[0] - chunk * K_TILE, scores, NEGATIVE)
    return scores


def fold_tile(query, limits, carry, k_ref, vt_ref):
    def step(masked, chunk, carry):
        highest, total, accum = carry
        k_rows = tile_rows(chunk, K_TILE)
        scores = masked_scores(masked, chunk, k_ref[k_rows, :], query, limits)
        new_high = jnp.maximum(highest, jnp.max(scores, axis=0, keepdims=True))
        weights = jnp.exp(scores - new_high)
        factor = jnp.exp(highest - new_high)
        total = total * factor + jnp.sum(weights, axis=0, keepdims=True)
        accum = accum * factor + dot(vt_ref[:, k_rows], weights.astype(BF16), 1, 0)
        return new_high, total, accum

    return loop_chunks(step, limits, carry)


def attend_own_kernel(
    head_ref, slope_ref, runs_ref, own_ref,
    sorted_ref, q_ref, k_ref, v_ref, high_ref, total_ref, accum_ref,
    place_ref, vt_ref,
):
    sort_runs(runs_ref, sorted_ref, place_ref)
    lanes = slope_lanes(head_ref, slope_ref)
    for source in range(16):
        for half in range(2):
            query = own_ref[source, :RUN, pl.ds(half * HEAD_DIM, HEAD_DIM)].astype(F32)
            q_ref[run_rows(sorted_ref[RANK + source * 2 + half]), :] = jnp.concatenate(
                [(query * HEAD_DIM ** (-0.5)).astype(BF16), lanes], axis=1
            )
    sort_keys(runs_ref, sorted_ref, own_ref, 128, k_ref, v_ref)
    transpose_rows(v_ref, vt_ref)

    def tile_step(tile, unused):
        q_rows = tile_rows(tile, Q_TILE)
        carry = (
            jnp.full((1, Q_TILE), NEGATIVE, F32),
            jnp.zeros((1, Q_TILE), F32),
            jnp.zeros((HEAD_DIM, Q_TILE), F32),
        )
        limits = tile_limits(sorted_ref, tile, True)
        carry = fold_tile(q_ref[q_rows, :], limits, carry, k_ref, vt_ref)
        high_ref[:, q_rows], total_ref[:, q_rows], accum_ref[:, q_rows] = carry
        return unused

    for tile in range(HALF_ROWS // Q_TILE):
        tile_step(tile, 0)


def attend_other_kernel(
    own_sorted_ref, runs_ref, other_ref, q_ref, high_ref, total_ref, accum_ref,
    out_ref, sorted_ref, k_ref, v_ref, exact_ref, log_ref,
    place_ref, vt_ref, rows_ref,
):
    sort_runs(runs_ref, sorted_ref, place_ref)
    sort_keys(runs_ref, sorted_ref, other_ref, 0, k_ref, v_ref)
    transpose_rows(v_ref, vt_ref)

    def tile_step(tile, unused):
        q_rows = tile_rows(tile, Q_TILE)
        carry = (high_ref[:, q_rows], total_ref[:, q_rows], accum_ref[:, q_rows])
        limits = tile_limits(own_sorted_ref, tile, False)
        highest, total, accum = fold_tile(q_ref[q_rows, :], limits, carry, k_ref, vt_ref)
        exact = accum / total
        exact_ref[:, q_rows] = exact
        log_ref[:, q_rows] = highest + jnp.log(total)
        rows_ref[q_rows, :] = exact.T
        return unused

    lax.fori_loop(0, HALF_ROWS // Q_TILE, tile_step, 0)
    for source in range(16):
        out_ref[source] = jnp.concatenate(
            [rows_ref[run_rows(own_sorted_ref[RANK + source * 2 + half]), :] for half in range(2)],
            axis=1,
        ).astype(BF16)


def unfold_tile(query, d_out, logs, delta, limits, dq, k_ref, v_ref, kt_ref, dk_ref, dv_ref):
    def step(masked, chunk, dq):
        k_rows = tile_rows(chunk, K_TILE)
        scores = masked_scores(masked, chunk, k_ref[k_rows, :], query, limits)
        weights = jnp.exp(scores - logs)
        d_weights = dot(v_ref[k_rows, :], d_out, 1, 1)
        d_scores = (weights * (d_weights - delta)).astype(BF16)
        dv_ref[k_rows, :] += dot(weights.astype(BF16), d_out, 1, 0)
        dk_ref[k_rows, :] += dot(d_scores, query, 1, 0)
        return dq + dot(kt_ref[:, k_rows], d_scores, 1, 0)

    return loop_chunks(step, limits, dq)


def write_keys(sorted_ref, dk_ref, dv_ref, target):
    for source in range(16):
        parts = []
        for half in range(2):
            place = run_rows(sorted_ref[RANK + source * 2 + half])
            parts += [dk_ref[place, :HEAD_DIM], dv_ref[place, :]]
        target[source] = jnp.concatenate(parts, axis=1).astype(target.dtype)


def back_other_kernel(
    own_sorted_ref, sorted_ref, grad_ref, q_ref, k_ref, v_ref, exact_ref, log_ref,
    other_out, dq_ref, do_ref, delta_ref,
    kt_ref, dk_ref, dv_ref,
):
    for source in range(16):
        for half in range(2):
            do_ref[run_rows(own_sorted_ref[RANK + source * 2 + half]), :] = grad_ref[
                source, :, pl.ds(half * HEAD_DIM, HEAD_DIM)
            ]
    transpose_rows(k_ref, kt_ref)
    dk_ref[...] = jnp.zeros_like(dk_ref)
    dv_ref[...] = jnp.zeros_like(dv_ref)

    def tile_step(tile, unused):
        q_rows = tile_rows(tile, Q_TILE)
        d_out = do_ref[q_rows, :]
        delta = jnp.sum(d_out.astype(F32).T * exact_ref[:, q_rows], axis=0, keepdims=True)
        delta_ref[:, q_rows] = delta
        dq_ref[:, q_rows] = unfold_tile(
            q_ref[q_rows, :], d_out, log_ref[:, q_rows], delta,
            tile_limits(own_sorted_ref, tile, False), jnp.zeros((HEAD_DIM, Q_TILE), F32),
            k_ref, v_ref, kt_ref, dk_ref, dv_ref,
        )
        return unused

    lax.fori_loop(0, HALF_ROWS // Q_TILE, tile_step, 0)
    write_keys(sorted_ref, dk_ref, dv_ref, other_out)


def back_own_kernel(
    sorted_ref, do_ref, q_ref, k_ref, v_ref, delta_ref, log_ref, dq_ref,
    dq_out, own_out,
    kt_ref, rows_ref, dk_ref, dv_ref,
):
    transpose_rows(k_ref, kt_ref)
    dk_ref[...] = jnp.zeros_like(dk_ref)
    dv_ref[...] = jnp.zeros_like(dv_ref)

    def tile_step(tile, unused):
        q_rows = tile_rows(tile, Q_TILE)
        dq = unfold_tile(
            q_ref[q_rows, :], do_ref[q_rows, :], log_ref[:, q_rows], delta_ref[:, q_rows],
            tile_limits(sorted_ref, tile, True), dq_ref[:, q_rows],
            k_ref, v_ref, kt_ref, dk_ref, dv_ref,
        )
        rows_ref[q_rows, :] = (dq * HEAD_DIM ** (-0.5)).T
        return unused

    for tile in range(HALF_ROWS // Q_TILE):
        tile_step(tile, 0)
    for source in range(16):
        dq_out[source] = jnp.concatenate(
            [rows_ref[run_rows(sorted_ref[RANK + source * 2 + half]), :] for half in range(2)],
            axis=1,
        ).astype(BF16)
    write_keys(sorted_ref, dk_ref, dv_ref, own_out)


def shape(*dims, dtype=F32):
    return jax.ShapeDtypeStruct(dims, dtype)


def call_attention(kernel, args, outs, scratch, smem):
    return pl.pallas_call(
        kernel,
        out_shape=outs,
        in_specs=[SMEM] * smem + [VMEM] * (len(args) - smem),
        out_specs=tuple(SMEM if out.dtype == jnp.int32 else VMEM for out in outs),
        scratch_shapes=scratch,
        compiler_params=PARAMS,
        cost_estimate=pl.CostEstimate(
            flops=12_000_000_000, bytes_accessed=4_000_000, transcendentals=4_000_000
        ),
    )(*args)


Q_SHAPE = shape(HALF_ROWS, 128, dtype=BF16)
V_SHAPE = shape(HALF_ROWS, HEAD_DIM, dtype=BF16)
ROW_SHAPE = shape(1, HALF_ROWS)
COLUMN_SHAPE = shape(HEAD_DIM, HALF_ROWS)
FLIPPED = pltpu.VMEM((HEAD_DIM, HALF_ROWS), BF16)
NARROW = pltpu.VMEM((HALF_ROWS, HEAD_DIM), F32)
WIDE = pltpu.VMEM((HALF_ROWS, 128), F32)


SORTED_SHAPE = shape(SORTED, dtype=jnp.int32)
PLACES = pltpu.SMEM((64,), jnp.int32)


def attend_own(*args):
    outs = (SORTED_SHAPE, Q_SHAPE, Q_SHAPE, V_SHAPE, ROW_SHAPE, ROW_SHAPE, COLUMN_SHAPE)
    return call_attention(attend_own_kernel, args, outs, [PLACES, FLIPPED], 3)


def attend_other(*args):
    outs = (shape(16, RUN, 128, dtype=BF16), SORTED_SHAPE, Q_SHAPE, V_SHAPE, COLUMN_SHAPE, ROW_SHAPE)
    return call_attention(attend_other_kernel, args, outs, [PLACES, FLIPPED, NARROW], 2)


def back_other(*args):
    outs = (shape(16, RUN, 256, dtype=BF16), COLUMN_SHAPE, V_SHAPE, ROW_SHAPE)
    return call_attention(back_other_kernel, args, outs, [FLIPPED, WIDE, NARROW], 2)


def back_own(*args):
    outs = (shape(16, RUN, 128, dtype=BF16), shape(16, RUN, 256))
    return call_attention(back_own_kernel, args, outs, [FLIPPED, NARROW, WIDE, NARROW], 1)


PLANES = [[2 * i + z for i in range(16)] for z in range(2)]


def swap(value, slot):
    return lax.ppermute(value, "wsh", [(i, i ^ slot) for i in range(4)])


def gather_list(value):
    across = swap(value, 2)
    return [value, swap(value, 1), across, swap(across, 1)]


def gather_slots(value):
    return jnp.concatenate(gather_list(value), axis=0)


def swap_weight(weight, rank, starts, size):
    def columns(slot, row, rows):
        parts = [
            lax.dynamic_slice(
                weight, (row, start + jnp.bitwise_xor(rank, slot) * size), (rows, size)
            )
            for start in starts
        ]
        return jnp.concatenate(parts, axis=1) if len(parts) > 1 else parts[0]

    pieces = [columns(0, 0, 256), columns(1, 0, 256)]
    pieces += [columns(slot, row, 128) for slot in (2, 3) for row in (0, 128)]
    return pieces


def swap_pieces(pieces):
    def wrapped(slot):
        return [(c * 4 + r, (c ^ 1) * 4 + (r ^ slot)) for c in range(32) for r in range(4)]

    return [
        pieces[0], swap(pieces[1], 1),
        swap(pieces[2], 2), lax.ppermute(pieces[3], ("ctx", "wsh"), wrapped(2)),
        swap(pieces[4], 3), lax.ppermute(pieces[5], ("ctx", "wsh"), wrapped(3)),
    ]


def reduce_slots(partial):
    rows = partial.reshape(4, 128, -1)
    across = rows[2] + swap(rows[3].astype(BF16), 1).astype(F32)
    across = swap(across.astype(BF16), 2).astype(F32)
    return rows[0] + swap(rows[1].astype(BF16), 1).astype(F32) + across


def in_order(slots, rank):
    return [
        lax.dynamic_index_in_dim(slots, jnp.bitwise_xor(rank, i), 0, keepdims=False)
        for i in range(4)
    ]


def head_exchange(value):
    return lax.all_to_all(value, "ctx", 0, 0, axis_index_groups=PLANES, tiled=True)


def partner(value):
    return lax.ppermute(value, "ctx", [(i, i ^ 1) for i in range(32)])


def plane_sum(received):
    total = jnp.sum(received.astype(F32), axis=0).astype(BF16)
    return total.astype(F32) + partner(total).astype(F32)


def plane_gather(shard):
    return lax.all_gather(shard, "ctx", axis=0, axis_index_groups=PLANES)


def spread(shard):
    rows = jnp.broadcast_to(shard, (16,) + shard.shape)
    return head_exchange(rows).reshape(rows.shape)


def body(
    tokens,
    places,
    w_qkv,
    b_qv,
    w_out,
    b_out,
    norm1_gain,
    norm1_shift,
    norm2_gain,
    norm2_shift,
    w_up,
    b_up,
    w_down,
    b_down,
    cotangent,
):
    rank = lax.axis_index("wsh")
    column = lax.axis_index("ctx")
    head = rank * 4 + (column // 2) % 4
    rank_scalar = rank.astype(jnp.int32).reshape(1)

    pieces = swap_weight(w_qkv, rank, (0, 1024, 2048), 256)
    vectors = (b_qv, b_out, norm1_gain, norm1_shift, norm2_gain, norm2_shift, b_up, b_down)
    pieces, vectors, places = lax.optimization_barrier((pieces, vectors, places))
    pieces = swap_pieces(pieces)
    runs = (places[0].reshape(2, RUN)[:, 0] // RUN).astype(BF16)
    small = [item.reshape(-1, 128) for item in vectors]
    small = jnp.concatenate(small + [jnp.pad(runs.reshape(1, 2), ((0, 0), (0, 126)))], axis=0)
    smalls = [small] + [swap(small, slot) for slot in (1, 2, 3)]
    smalls, w_up, cotangent = lax.optimization_barrier((smalls, w_up, cotangent))
    packed, normed_one, part_qkv, vector = start(
        rank_scalar, gather_list(tokens[0]), pieces, smalls
    )
    full_bout = vector[0, 2048:3072]
    gain_one = vector[0, 3072:4096]
    shift_one = vector[0, 4096:5120]
    gain_two = vector[0, 5120:6144]
    shift_two = vector[0, 6144:7168]
    bias_up = lax.dynamic_slice_in_dim(vector, 7168 + rank * 1024, 1024, 1)
    full_bdown = vector[0, 11264:]

    own = head_exchange(packed)

    up_pieces = swap_pieces(swap_weight(w_up, rank, (0,), 1024))
    d_down = gather_list(cotangent[0])

    def run_indices(message):
        return message[:, RUN, :2].astype(jnp.int32).reshape(32)

    other = partner(own[:, :, 128:])
    own_sorted, q, k_own, v_own, *state = attend_own(
        head.astype(jnp.int32).reshape(1), slope_table(), run_indices(own), own
    )
    out_packed, other_sorted, k_other, v_other, exact, logs = attend_other(
        own_sorted, run_indices(other), other, q, *state
    )
    out_packed, up_pieces, d_down = lax.optimization_barrier((out_packed, up_pieces, d_down))
    up_slots = [
        up_pieces[0], up_pieces[1],
        jnp.concatenate(up_pieces[2:4], axis=0), jnp.concatenate(up_pieces[4:], axis=0),
    ]
    part_up = jnp.concatenate(in_order(jnp.stack(up_slots), rank), axis=0)
    d_down = jnp.concatenate(d_down, axis=0)
    attended = unpack_heads(head_exchange(out_packed))

    def to_owners(pieces, parts):
        slots = pieces.astype(BF16).reshape(4, 16, -1)
        slots = jnp.stack([slots[0]] + [swap(slots[s], s) for s in (1, 2, 3)])
        columns = jnp.stack(in_order(slots, rank))
        return columns if parts == 1 else columns.reshape(4, 16, parts, -1)

    residual_in = tokens[0].astype(F32)
    middle = residual_in + reduce_slots(dot(attended, w_out, 1, 0)) + full_bout
    normed_two, norm_two_back = jax.vjp(layer_norm, middle, gain_two, shift_two)
    normed_two = gather_slots(normed_two.astype(BF16))
    pre_act = dot(normed_two, part_up, 1, 0) + bias_up
    hidden, gelu_back = jax.vjp(gelu_tanh, pre_act)
    hidden = hidden.astype(BF16)
    grad_wdown = dot(hidden, d_down, 0, 0).astype(BF16).reshape(16, 64, 1024)

    d_output_slots, grad_wdown = lax.optimization_barrier((d_down, grad_wdown))
    grad_wdown = head_exchange(grad_wdown)
    (d_pre,) = gelu_back(dot(d_output_slots, w_down, 1, 1))
    d_pre = d_pre.astype(BF16)
    d_normed_two = reduce_slots(dot(d_pre, part_up, 1, 1))
    d_norm_two, grad_gain_two, grad_shift_two = norm_two_back(d_normed_two)
    d_output = cotangent[0].astype(F32)
    d_middle = d_output + d_norm_two
    d_branch_own = d_middle.astype(BF16)
    d_branch = gather_slots(d_branch_own)
    d_attended = dot(d_branch, w_out, 1, 1)

    d_packed, grad_wdown = lax.optimization_barrier((pack_heads(d_attended), grad_wdown))
    grad = head_exchange(d_packed)
    early = early_pieces(rank_scalar, normed_two, d_pre, attended, d_branch)
    grad, early = lax.optimization_barrier((grad, early))
    early = head_exchange(early)
    grad_wdown = plane_gather(plane_sum(grad_wdown).astype(BF16))
    dkv_other, dq, d_out, delta = back_other(
        own_sorted, other_sorted, grad, q, k_other, v_other, exact, logs
    )
    dkv_other = partner(dkv_other)
    dq, dkv_own = back_own(own_sorted, d_out, q, k_own, v_own, delta, logs, dq)
    dkv = (dkv_own + dkv_other.astype(F32)).astype(BF16)
    d_packed = jnp.concatenate([dq, dkv], axis=2)
    d_packed, early, hidden = lax.optimization_barrier((d_packed, early, hidden))
    d_packed = head_exchange(d_packed)
    output = middle + reduce_slots(dot(hidden, w_down, 1, 0)) + full_bdown
    early = plane_sum(early)
    up_rows = to_owners(early[:64], 1).reshape(64, 1024)
    early = plane_gather(jnp.concatenate([up_rows, early[64:].astype(BF16)], axis=0))
    d_packed, grad_wdown = lax.optimization_barrier((d_packed, grad_wdown))
    d_mixed, late = late_pieces(rank_scalar, d_packed, normed_one)
    late = head_exchange(late)
    d_normed_one = reduce_slots(dot(d_mixed, part_qkv, 1, 1))
    _, norm_one_back = jax.vjp(layer_norm, residual_in, gain_one, shift_one)
    d_norm_one, grad_gain_one, grad_shift_one = norm_one_back(d_normed_one)
    grad_input = d_middle + d_norm_one

    sums = jnp.sum(d_mixed.astype(F32), axis=0)
    grad_bqv = jnp.zeros((2048,), F32)
    grad_bqv = lax.dynamic_update_slice_in_dim(grad_bqv, sums[:256], rank * 256, 0)
    grad_bqv = lax.dynamic_update_slice_in_dim(grad_bqv, sums[512:], 1024 + rank * 256, 0)
    grad_bup = lax.dynamic_update_slice_in_dim(
        jnp.zeros((4, 1024), F32), jnp.sum(d_pre.astype(F32), axis=0)[None], rank, 0
    )
    vectors = jnp.concatenate(
        [
            grad_bqv.reshape(4, 512),
            jnp.sum(d_branch_own.astype(F32), axis=0).reshape(4, 256),
            grad_gain_one.reshape(4, 256),
            grad_shift_one.reshape(4, 256),
            grad_gain_two.reshape(4, 256),
            grad_shift_two.reshape(4, 256),
            grad_bup,
            jnp.sum(d_output, axis=0).reshape(4, 256),
        ],
        axis=1,
    )
    vectors = jnp.stack(in_order(vectors, rank)).reshape(4, 24, 128).astype(BF16)
    vectors = vectors.astype(F32) + partner(vectors).astype(F32)
    vector = vectors[0]
    for slot in (1, 2, 3):
        vector = vector + swap(vectors[slot].astype(BF16), slot).astype(F32)
    late, vector = lax.optimization_barrier((late, vector))
    late = to_owners(plane_sum(late), 3).reshape(4, 16, 3, 2, 128)
    late = late.transpose(2, 0, 3, 1, 4).reshape(384, 128)
    vector = jnp.pad(vector.astype(BF16), ((0, 8), (0, 0)))
    late = spread(jnp.concatenate([late, vector], axis=0))

    out_wdown = grad_wdown.reshape(1024, 1024).astype(F32)
    out_wup, out_wout = spread_early(early)
    late, out_wup, out_wout = lax.optimization_barrier((late, out_wup, out_wout))
    out_wqkv, out_vec = spread_late(late)
    out_vec = out_vec[:24].reshape(3072)
    return (
        output.astype(BF16)[None],
        grad_input.astype(BF16)[None],
        out_wqkv,
        out_vec[0:512],
        out_wout,
        out_vec[512:768],
        out_vec[768:1024],
        out_vec[1024:1280],
        out_vec[1280:1536],
        out_vec[1536:1792],
        out_wup,
        out_vec[1792:2816],
        out_wdown,
        out_vec[2816:3072],
    )


def solution(mesh):
    rows = P("wsh", "ctx", None)
    matrix = P("wsh", None)
    vector = P("wsh")
    return jax.shard_map(
        body,
        mesh=mesh,
        in_specs=(
            rows, P("wsh", "ctx"), matrix, vector, matrix, vector, vector, vector, vector, vector,
            matrix, vector, matrix, vector, rows,
        ),
        out_specs=(
            rows, rows, matrix, vector, matrix, vector, vector, vector, vector, vector,
            matrix, vector, matrix, vector,
        ),
        check_vma=False,
    )
```
